128 devices in a mesh: gy: 8 (over z_hi, y), gz: 16 (over z_lo, x, core).
Axes of the slice: x: 4, y: 4, z: 4 (z_hi: 2, z_lo: 2; z = z_hi * 2 + z_lo), core: 2. Of those that a mesh axis runs over, the one named last changes fastest.
Arguments:
- eigenvectors: bfloat16 [1, 64, 64, 16, 2, 3, 128], P(None, 'gy', 'gz'), may hold values from -6 to 6
- gauge_links: float32 [1, 3, 2, 3, 3, 64, 64, 16], P(None, None, None, None, None, 'gy', 'gz'), may hold values from -3 to 3
Outputs:
- elementals: float32 [128, 1, 4, 2, 128], P(('gy', 'gz'))
The draws below stay inside these ranges and needn't reach their ends.
All inputs are finite; a program needn't handle non-finite values.
Results may differ from the reference program's by a relative error of at most 0.0028.
Values may be sent and summed in bfloat16 or wider, within the bound.
No kernel may reach another device: no remote copies, remote signals or barrier semaphores. Data moves between devices by JAX's collectives and lax.ppermute only.
A program may use at most 64 MiB of HBM per device.

```python
import math
import jax
import jax.numpy as jnp
from jax import lax

NVEC = 128
TS = 1
NX = 16
NY = 64
NZ = 64


def levels(rng, extent, cuts, smallest, largest):
    loudness = 1.0
    for axis_at, parts in cuts:
        heights = jax.random.uniform(jax.random.fold_in(jax.random.fold_in(rng, 6), axis_at), (parts,), jnp.float32, smallest / len(cuts), largest / len(cuts))
        loudness = loudness * jnp.repeat(jnp.exp(heights), extent[axis_at] // parts).reshape((-1,) + (1,) * (len(extent) - 1 - axis_at))
    return loudness


def normal_values(rng, dims, spread, bound, cuts=(), kind=jnp.bfloat16):
    result = spread * jax.random.normal(rng, dims, jnp.float32)
    if cuts:
        result = result * levels(rng, dims, cuts, -0.22, 0.18)
    return jnp.clip(result, -bound, bound).astype(kind)


def setup_inputs(seed: int = 0) -> dict:
    key_of = jax.random.split(jax.random.key(seed), 3)
    return {
        "eigenvectors": normal_values(key_of[0], (TS, NY, NZ, NX, 2, 3, NVEC), 1.0, 6.0, ((1, 8), (2, 16))),
        "gauge_links": normal_values(key_of[1], (TS, 3, 2, 3, 3, NY, NZ, NX), 0.6, 3.0, ((5, 8), (6, 16)), jnp.float32),
    }


def transport(link_dir, source, dagger):
    link_real = jnp.transpose(link_dir[0], (2, 3, 4, 0, 1))
    link_imag = jnp.transpose(link_dir[1], (2, 3, 4, 0, 1))
    if dagger:
        link_real = jnp.swapaxes(link_real, 3, 4)
        link_imag = -jnp.swapaxes(link_imag, 3, 4)
    vec_real = source[:, :, :, 0].astype(jnp.float32)
    vec_imag = source[:, :, :, 1].astype(jnp.float32)
    out_real = jnp.zeros(vec_real.shape, jnp.float32)
    out_imag = jnp.zeros(vec_real.shape, jnp.float32)
    for colour in range(3):
        coef_real = link_real[:, :, :, :, colour][..., None]
        coef_imag = link_imag[:, :, :, :, colour][..., None]
        part_real = vec_real[:, :, :, colour:colour + 1, :]
        part_imag = vec_imag[:, :, :, colour:colour + 1, :]
        out_real = out_real + coef_real * part_real - coef_imag * part_imag
        out_imag = out_imag + coef_real * part_imag + coef_imag * part_real
    return jnp.stack([out_real, out_imag], axis=3)


def rotate(source):
    count = source.shape[2]
    angles = jnp.arange(count, dtype=jnp.float32) * (2.0 * math.pi / count)
    cosine = jnp.cos(angles)[None, None, :, None, None]
    sine = -jnp.sin(angles)[None, None, :, None, None]
    vec_real = source[:, :, :, 0].astype(jnp.float32)
    vec_imag = source[:, :, :, 1].astype(jnp.float32)
    out_real = cosine * vec_real - sine * vec_imag
    out_imag = cosine * vec_imag + sine * vec_real
    return jnp.stack([out_real, out_imag], axis=3)


def elemental(left_block, image):
    width = left_block.shape[-1]
    swapped = jnp.stack([image[:, :, :, 1], -image[:, :, :, 0]], axis=3)
    right_block = jnp.concatenate([image, swapped], axis=-1)
    product = lax.dot_general(left_block.reshape(-1, width), right_block.reshape(-1, 2 * width), (((0,), (0,)), ((), ())), preferred_element_type=jnp.float32)
    return product.reshape(width, 2, width)


def reference(eigenvectors, gauge_links):
    norm_factor = (6.0 * NX * NY * NZ) ** -0.5
    per_slice = []
    for slice_index in range(TS):
        source = eigenvectors[slice_index]
        links_now = gauge_links[slice_index]
        images = [rotate(source).astype(jnp.bfloat16)]
        for direction in range(3):
            axis_pos = 2 if direction == 0 else direction - 1
            link_dir = links_now[direction]
            ahead = transport(link_dir, jnp.roll(source, -1, axis_pos), False)
            behind = transport(jnp.roll(link_dir, 1, axis=3 + axis_pos), jnp.roll(source, 1, axis_pos), True)
            images.append((0.5 * (ahead - behind)).astype(jnp.bfloat16))
        stacked = jnp.stack([elemental(source, image) for image in images], axis=1)
        per_slice.append(stacked * norm_factor)
    return jnp.stack(per_slice, axis=1)
```

```python
import functools

import jax
import jax.numpy as jnp
import ml_dtypes
import numpy as np
from jax import lax
from jax.experimental import pallas as pl
from jax.experimental.pallas import tpu as pltpu
from jax.sharding import PartitionSpec as P

BF16 = ml_dtypes.bfloat16


def split(value):
    high = value.astype(BF16)
    low = (value - high.astype(np.float32)).astype(BF16)
    return high, low


def row_at(x, colour, part):
    return (x * 3 + colour) * 2 + part


def constants(count):
    rows = 6 * count
    swap = np.zeros((rows, rows), np.float32)
    spin = np.zeros((rows, rows), np.float32)
    angles = np.arange(count, dtype=np.float32) * np.float32(2.0 * np.pi / count)
    cosine, sine = np.cos(angles), -np.sin(angles)
    for x in range(count):
        for colour in range(3):
            re, im = row_at(x, colour, 0), row_at(x, colour, 1)
            swap[re, im], swap[im, re] = -1.0, 1.0
            spin[re, re], spin[re, im] = cosine[x], -sine[x]
            spin[im, im], spin[im, re] = cosine[x], sine[x]
    fixed = np.zeros((2, rows, 2, 128), BF16)
    fixed[0, :, 0, :rows] = swap.astype(BF16)
    fixed[1, :, 0, :rows], fixed[1, :, 1, :rows] = split(spin)
    spread = np.zeros((2, 2, 128, 2, 2, 128), np.float32)
    masks = np.zeros((2, rows, 2, 128), np.float32)
    for shift in range(2):
        for x in range(count):
            there = (x + shift) % count
            for colour in range(3):
                for part in range(2):
                    for to_part in range(2):
                        lane = ((part ^ to_part) * 3 + colour) * count + x
                        sign = -1.0 if (part, to_part) == (0, 1) else 1.0
                        for half in range(2):
                            spread[shift, half, lane, part, half, row_at(there, colour, to_part)] = sign
            masks[shift, 6 * x : 6 * x + 6, :, 6 * there : 6 * there + 6] = 1.0
    return (
        fixed.reshape(2 * rows, 256),
        spread.reshape(2, 256, 512).astype(BF16),
        masks.reshape(2, rows, 256).astype(BF16),
    )


def kernel(
    slab_y, slab_z, count, scale, v_ref, face_y, face_z, links, fixed, spread, masks, out,
    coefs, left, right,
):
    rows = 6 * count
    sites = slab_y * slab_z
    width = v_ref.shape[1]

    def link(direction, part, colour, other):
        start = (((direction * 2 + part) * 3 + colour) * 3 + other) * sites
        return links[pl.ds(start, sites), :]

    for direction in range(3):
        flat = []
        for colour in range(3):
            pieces = [link(direction, part, colour, other) for part in range(2) for other in range(3)]
            pieces.append(jnp.zeros((sites, 128 - 6 * count), jnp.float32))
            flat.append(jnp.concatenate(pieces, axis=1))
        flat = jnp.concatenate(flat, axis=0)
        high = flat.astype(jnp.bfloat16)
        low = (flat - high.astype(jnp.float32)).astype(jnp.bfloat16)
        wide = jnp.dot(
            jnp.concatenate([high, low], axis=1),
            spread[1 if direction == 0 else 0],
            preferred_element_type=jnp.float32,
        )
        for colour in range(3):
            for part in range(2):
                for half in range(2):
                    lane = (part * 2 + half) * 128
                    value = wide[colour * sites : (colour + 1) * sites, lane : lane + 128]
                    for copy in range(4):
                        first = (half * 3 + direction) * sites * 24 + copy * 6 + colour * 2 + part
                        coefs[pl.ds(first, sites, stride=24), :] = value

    def matrix(direction, site):
        halves = []
        for half in range(2):
            start = pl.multiple_of(((half * 3 + direction) * sites + site) * 24, 24)
            value = coefs[pl.ds(start, 24), :]
            value = jnp.concatenate([value, value], axis=0).astype(jnp.bfloat16)
            halves.append(jnp.concatenate([value] * (rows // 48), axis=0))
        return jnp.concatenate(halves, axis=1) * masks[1 if direction == 0 else 0]

    def apply(matrices, source):
        padding = jnp.zeros((128 - rows, width), source.dtype)
        return jnp.dot(
            jnp.concatenate(matrices, axis=0),
            jnp.concatenate([source, padding, source, padding], axis=0),
            preferred_element_type=jnp.float32,
        ).astype(jnp.bfloat16)

    def at(site):
        return pl.ds(pl.multiple_of(site * rows, rows), rows)

    def step(y, _):
        for z in range(slab_z):
            site = y * slab_z + z
            source = v_ref[at(site), :]
            behind_y = jnp.maximum(y - 1, 0) * slab_z + z
            matrices = [fixed[...], matrix(0, site), matrix(1, behind_y)]
            if z > 0:
                matrices.append(matrix(2, site - 1))
            images = apply(matrices, source)
            left[at(site), :width] = source
            left[at(site), width:] = images[:rows]
            right[at(site), : 2 * width] = jnp.concatenate(
                [images[rows : 2 * rows], images[2 * rows : 3 * rows]], axis=1
            )
            right[at(behind_y), 2 * width : 3 * width] = images[3 * rows : 4 * rows]
            if z > 0:
                right[at(site - 1), 3 * width :] = images[4 * rows :]
        edge = y * slab_z + slab_z - 1
        right[at(edge), 3 * width :] = apply([matrix(2, edge)], face_z[at(y), :])
        return 0

    lax.fori_loop(0, slab_y, step, 0)
    for z in range(slab_z):
        edge = (slab_y - 1) * slab_z + z
        right[at(edge), 2 * width : 3 * width] = apply([matrix(1, edge)], face_y[at(z), :])

    total = lax.dot_general(
        left[...], right[...], (((0,), (0,)), ((), ())), preferred_element_type=jnp.float32
    )
    for operator in range(4):
        real = total[:width, operator * width : (operator + 1) * width]
        imag = total[width:, operator * width : (operator + 1) * width]
        if operator == 0:
            real, imag = real * scale, imag * scale
        else:
            real, imag = (real - real.T) * (0.5 * scale), (imag + imag.T) * (0.5 * scale)
        out[pl.ds(operator, width, stride=8), :] = real
        out[pl.ds(4 + operator, width, stride=8), :] = imag


def shifted(block, axis):
    size = lax.axis_size(axis)
    return lax.ppermute(block, axis, [((i + 1) % size, i) for i in range(size)])


def per_device(eigenvectors, gauge_links):
    _, slab_y, slab_z, count, _, _, width = eigenvectors.shape
    rows = 6 * count
    sites = slab_y * slab_z
    scale = (6.0 * count * slab_y * lax.axis_size("gy") * slab_z * lax.axis_size("gz")) ** (-0.5)
    field = jnp.transpose(eigenvectors[0], (0, 1, 2, 4, 3, 5)).reshape(slab_y, slab_z, rows, width)
    face_z = shifted(field[:, 0].reshape(slab_y * rows, width), "gz")
    face_y = shifted(field[0].reshape(slab_z * rows, width), "gy")
    fixed, spread, masks = constants(count)
    partial = pl.pallas_call(
        functools.partial(kernel, slab_y, slab_z, count, scale),
        out_shape=jax.ShapeDtypeStruct((8 * width, width), jnp.float32),
        scratch_shapes=[
            pltpu.VMEM((6 * sites * 24, 128), jnp.float32),
            pltpu.VMEM((sites * rows, 2 * width), jnp.bfloat16),
            pltpu.VMEM((sites * rows, 4 * width), jnp.bfloat16),
        ],
        compiler_params=pltpu.CompilerParams(vmem_limit_bytes=48 * 1024 * 1024),
    )(
        field.reshape(sites * rows, width),
        face_y,
        face_z,
        gauge_links.reshape(54 * sites, count),
        fixed,
        spread,
        masks,
    )
    gathered = lax.all_to_all(partial.reshape(width, 8, width), ("gy", "gz"), 0, 0, tiled=True)
    mine = jnp.sum(gathered, axis=0)
    return jnp.transpose(mine.reshape(2, 4, width), (1, 0, 2))[None, None]


def solution(mesh):
    placed = (
        P(None, "gy", "gz", None, None, None, None),
        P(None, None, None, None, None, "gy", "gz", None),
    )
    return jax.shard_map(
        per_device,
        mesh=mesh,
        in_specs=placed,
        out_specs=P(("gy", "gz"), None, None, None, None),
        check_vma=False,
    )
```

```python
import functools

import jax
import jax.numpy as jnp
import ml_dtypes
import numpy as np
from jax import lax
from jax.experimental import pallas as pl
from jax.experimental.pallas import tpu as pltpu
from jax.sharding import PartitionSpec as P

BF16 = ml_dtypes.bfloat16


def split(value):
    high = value.astype(BF16)
    low = (value - high.astype(np.float32)).astype(BF16)
    return high, low


def row_at(x, colour, part):
    return (x * 3 + colour) * 2 + part


def constants(count):
    rows = 6 * count
    swap = np.zeros((rows, rows), np.float32)
    spin = np.zeros((rows, rows), np.float32)
    angles = np.arange(count, dtype=np.float32) * np.float32(2.0 * np.pi / count)
    cosine, sine = np.cos(angles), -np.sin(angles)
    for x in range(count):
        for colour in range(3):
            re, im = row_at(x, colour, 0), row_at(x, colour, 1)
            swap[re, im], swap[im, re] = -1.0, 1.0
            spin[re, re], spin[re, im] = cosine[x], -sine[x]
            spin[im, im], spin[im, re] = cosine[x], sine[x]
    fixed = np.zeros((2, rows, 2, 128), BF16)
    fixed[0, :, 0, :rows] = swap.astype(BF16)
    fixed[1, :, 0, :rows], fixed[1, :, 1, :rows] = split(spin)
    spread = np.zeros((2, 2, 128, 2, 2, 128), np.float32)
    masks = np.zeros((2, rows, 2, 128), np.float32)
    for shift in range(2):
        for x in range(count):
            there = (x + shift) % count
            for colour in range(3):
                for part in range(2):
                    for to_part in range(2):
                        lane = ((part ^ to_part) * 3 + colour) * count + x
                        sign = -1.0 if (part, to_part) == (0, 1) else 1.0
                        for half in range(2):
                            spread[shift, half, lane, part, half, row_at(there, colour, to_part)] = sign
            masks[shift, 6 * x : 6 * x + 6, :, 6 * there : 6 * there + 6] = 1.0
    return (
        fixed.reshape(2 * rows, 256),
        spread.reshape(2, 256, 512).astype(BF16),
        masks.reshape(2, rows, 256).astype(BF16),
    )


def site_rows(site, rows):
    return pl.ds(pl.multiple_of(site * rows, rows), rows)


def spread_links(flat, spread):
    high = flat.astype(jnp.bfloat16)
    low = (flat - high.astype(jnp.float32)).astype(jnp.bfloat16)
    return jnp.dot(
        jnp.concatenate([high, low], axis=1), spread, preferred_element_type=jnp.float32
    )


def store_coefs(coefs, base, stride, wide, sites):
    for colour in range(3):
        for part in range(2):
            for half in range(2):
                lane = (part * 2 + half) * 128
                value = wide[colour * sites : (colour + 1) * sites, lane : lane + 128]
                for copy in range(4):
                    first = base + half * stride + copy * 6 + colour * 2 + part
                    coefs[pl.ds(first, sites, stride=24), :] = value


def block_matrix(coefs, start, stride, rows, mask):
    halves = []
    for half in range(2):
        value = coefs[pl.ds(pl.multiple_of(start + half * stride, 24), 24), :]
        value = jnp.concatenate([value, value], axis=0).astype(jnp.bfloat16)
        halves.append(jnp.concatenate([value] * (rows // 48), axis=0))
    return jnp.concatenate(halves, axis=1) * mask


def apply(matrices, source):
    rows, width = source.shape
    padding = jnp.zeros((128 - rows, width), source.dtype)
    return jnp.dot(
        jnp.concatenate(matrices, axis=0),
        jnp.concatenate([source, padding, source, padding], axis=0),
        preferred_element_type=jnp.float32,
    ).astype(jnp.bfloat16)


def faces_kernel(
    slab_y, slab_z, count, v_hbm, links_hbm, spread_hbm, masks_hbm, face_y, face_z,
    links, spread, masks, last_y, last_z, coefs, sems,
):
    rows = 6 * count
    sites = slab_y * slab_z
    used = 8 + sites
    moves = [
        pltpu.make_async_copy(links_hbm.at[pl.ds(18 * sites, 36 * sites)], links, sems.at[0]),
        pltpu.make_async_copy(spread_hbm.at[0], spread, sems.at[1]),
        pltpu.make_async_copy(masks_hbm.at[0], masks, sems.at[2]),
        pltpu.make_async_copy(
            v_hbm.at[pl.ds((slab_y - 1) * slab_z * rows, slab_z * rows)], last_y, sems.at[3]
        ),
    ]
    for y in range(slab_y):
        source = v_hbm.at[pl.ds((y * slab_z + slab_z - 1) * rows, rows)]
        moves.append(pltpu.make_async_copy(source, last_z.at[pl.ds(y * rows, rows)], sems.at[4 + y]))
    for move in moves:
        move.start()
    for move in moves[:2]:
        move.wait()
    for direction, first, number, base in ((1, sites - 8, 8, 0), (2, 0, sites, 8)):
        flat = []
        for other in range(3):
            pieces = []
            for part in range(2):
                for colour in range(3):
                    start = ((((direction - 1) * 2 + part) * 3 + colour) * 3 + other) * sites
                    piece = links[pl.ds(start + first, number), :]
                    pieces.append(-piece if part else piece)
            pieces.append(jnp.zeros((number, 128 - rows), jnp.float32))
            flat.append(jnp.concatenate(pieces, axis=1))
        wide = spread_links(jnp.concatenate(flat, axis=0), spread[...])
        store_coefs(coefs, base * 24, used * 24, wide, number)
    for move in moves[2:]:
        move.wait()
    mask = masks[...]
    for z in range(slab_z):
        matrix = block_matrix(coefs, (8 - slab_z + z) * 24, used * 24, rows, mask)
        face_y[site_rows(z, rows), :] = apply([matrix], last_y[site_rows(z, rows), :])
    for y in range(slab_y):
        matrix = block_matrix(coefs, (8 + y * slab_z + slab_z - 1) * 24, used * 24, rows, mask)
        face_z[site_rows(y, rows), :] = apply([matrix], last_z[site_rows(y, rows), :])


def local_kernel(
    slab_y, slab_z, count, v_ref, links, fixed, spread, masks, total, first_y, first_z,
    coefs, left, right,
):
    rows = 6 * count
    sites = slab_y * slab_z
    width = v_ref.shape[1]

    for direction in range(3):
        flat = []
        for colour in range(3):
            pieces = []
            for part in range(2):
                for other in range(3):
                    start = (((direction * 2 + part) * 3 + colour) * 3 + other) * sites
                    pieces.append(links[pl.ds(start, sites), :])
            pieces.append(jnp.zeros((sites, 128 - rows), jnp.float32))
            flat.append(jnp.concatenate(pieces, axis=1))
        wide = spread_links(jnp.concatenate(flat, axis=0), spread[1 if direction == 0 else 0])
        store_coefs(coefs, direction * sites * 24, 3 * sites * 24, wide, sites)

    def matrix(direction, site):
        start = (direction * sites + site) * 24
        return block_matrix(coefs, start, 3 * sites * 24, rows, masks[1 if direction == 0 else 0])

    def at(site):
        return site_rows(site, rows)

    def step(y):
        for z in range(slab_z):
            site = y * slab_z + z
            source = v_ref[at(site), :]
            matrices = [fixed[...], matrix(0, site)]
            if y > 0:
                matrices.append(matrix(1, site - slab_z))
            if z > 0:
                matrices.append(matrix(2, site - 1))
            images = apply(matrices, source)
            left[at(site), :width] = source
            left[at(site), width:] = images[:rows]
            right[at(site), : 2 * width] = jnp.concatenate(
                [images[rows : 2 * rows], images[2 * rows : 3 * rows]], axis=1
            )
            if y > 0:
                right[at(site - slab_z), 2 * width : 3 * width] = images[3 * rows : 4 * rows]
            if z > 0:
                right[at(site - 1), 3 * width :] = images[-rows:]
            else:
                first_z[at(y), :] = left[at(site), :]
        right[at(y * slab_z + slab_z - 1), 3 * width :] = jnp.zeros((rows, width), jnp.bfloat16)

    for y in range(slab_y):
        step(y)
    first_y[...] = left[pl.ds(0, slab_z * rows), :]
    last = pl.ds((slab_y - 1) * slab_z * rows, slab_z * rows)
    right[last, 2 * width : 3 * width] = jnp.zeros((slab_z * rows, width), jnp.bfloat16)
    total[...] = lax.dot_general(
        left[...], right[...], (((0,), (0,)), ((), ())), preferred_element_type=jnp.float32
    )


def edge_kernel(scale, total, first_y, first_z, face_y, face_z, out, sums):
    width = face_y.shape[1]

    def product(first, face):
        return lax.dot_general(
            first[...], face[...], (((0,), (0,)), ((), ())), preferred_element_type=jnp.float32
        )

    extra = {2: product(first_y, face_y), 3: product(first_z, face_z)}
    for operator in range(4):
        both = total[:, operator * width : (operator + 1) * width]
        if operator in extra:
            both = both - extra[operator]
        real, imag = both[:width], both[width:]
        if operator == 0:
            real, imag = real * scale, imag * scale
        else:
            real, imag = (real - real.T) * (0.5 * scale), (imag + imag.T) * (0.5 * scale)
        sums[pl.ds(2 * operator, width, stride=8), :] = real
        sums[pl.ds(2 * operator + 1, width, stride=8), :] = imag
    out[...] = sums[...].astype(jnp.bfloat16)


def shifted(block, axis):
    size = lax.axis_size(axis)
    return lax.ppermute(block, axis, [(i, (i + 1) % size) for i in range(size)])


def per_device(eigenvectors, gauge_links):
    _, slab_y, slab_z, count, _, _, width = eigenvectors.shape
    rows = 6 * count
    sites = slab_y * slab_z
    scale = (6.0 * count * slab_y * lax.axis_size("gy") * slab_z * lax.axis_size("gz")) ** (-0.5)
    field = jnp.transpose(eigenvectors[0], (0, 1, 2, 4, 3, 5)).reshape(sites * rows, width)
    links = gauge_links.reshape(54 * sites, count)
    fixed, spread, masks = constants(count)
    face_y, face_z = pl.pallas_call(
        functools.partial(faces_kernel, slab_y, slab_z, count),
        out_shape=[
            jax.ShapeDtypeStruct((slab_z * rows, width), jnp.bfloat16),
            jax.ShapeDtypeStruct((slab_y * rows, width), jnp.bfloat16),
        ],
        in_specs=[pl.BlockSpec(memory_space=pltpu.HBM)] * 4,
        scratch_shapes=[
            pltpu.VMEM((36 * sites, count), jnp.float32),
            pltpu.VMEM(spread.shape[1:], jnp.bfloat16),
            pltpu.VMEM(masks.shape[1:], jnp.bfloat16),
            pltpu.VMEM((slab_z * rows, width), jnp.bfloat16),
            pltpu.VMEM((slab_y * rows, width), jnp.bfloat16),
            pltpu.VMEM((2 * (8 + sites) * 24, 128), jnp.float32),
            pltpu.SemaphoreType.DMA((4 + slab_y,)),
        ],
        compiler_params=pltpu.CompilerParams(vmem_limit_bytes=60 * 1024 * 1024),
        cost_estimate=pl.CostEstimate(flops=10_000_000_000, bytes_accessed=600_000, transcendentals=0),
    )(field, links, spread, masks)
    face_y = shifted(face_y, "gy")
    face_z = shifted(face_z, "gz")
    total, first_y, first_z = pl.pallas_call(
        functools.partial(local_kernel, slab_y, slab_z, count),
        out_shape=[
            jax.ShapeDtypeStruct((2 * width, 4 * width), jnp.float32),
            jax.ShapeDtypeStruct((slab_z * rows, 2 * width), jnp.bfloat16),
            jax.ShapeDtypeStruct((slab_y * rows, 2 * width), jnp.bfloat16),
        ],
        scratch_shapes=[
            pltpu.VMEM((6 * sites * 24, 128), jnp.float32),
            pltpu.VMEM((sites * rows, 2 * width), jnp.bfloat16),
            pltpu.VMEM((sites * rows, 4 * width), jnp.bfloat16),
        ],
        compiler_params=pltpu.CompilerParams(vmem_limit_bytes=32 * 1024 * 1024),
        cost_estimate=pl.CostEstimate(flops=5_000_000_000, bytes_accessed=4_000_000, transcendentals=0),
    )(field, links, fixed, spread, masks)
    partial = pl.pallas_call(
        functools.partial(edge_kernel, scale),
        out_shape=jax.ShapeDtypeStruct((8 * width, width), jnp.bfloat16),
        scratch_shapes=[pltpu.VMEM((8 * width, width), jnp.float32)],
        compiler_params=pltpu.CompilerParams(vmem_limit_bytes=16 * 1024 * 1024),
    )(total, first_y, first_z, face_y, face_z)
    gathered = lax.all_to_all(partial.reshape(width, 8, width), ("gy", "gz"), 0, 0, tiled=True)
    return jnp.sum(gathered.astype(jnp.float32), axis=0).reshape(1, 1, 4, 2, width)


def solution(mesh):
    placed = (
        P(None, "gy", "gz", None, None, None, None),
        P(None, None, None, None, None, "gy", "gz", None),
    )
    return jax.shard_map(
        per_device,
        mesh=mesh,
        in_specs=placed,
        out_specs=P(("gy", "gz"), None, None, None, None),
        check_vma=False,
    )
```

```python
import functools

import jax
import jax.numpy as jnp
import ml_dtypes
import numpy as np
from jax import lax
from jax.experimental import pallas as pl
from jax.experimental.pallas import tpu as pltpu
from jax.sharding import PartitionSpec as P

BF16 = ml_dtypes.bfloat16


def split(value):
    high = value.astype(BF16)
    low = (value - high.astype(np.float32)).astype(BF16)
    return high, low


def row_at(x, colour, part):
    return (x * 3 + colour) * 2 + part


def constants(count):
    rows = 6 * count
    swap = np.zeros((rows, rows), np.float32)
    spin = np.zeros((rows, rows), np.float32)
    angles = np.arange(count, dtype=np.float32) * np.float32(2.0 * np.pi / count)
    cosine, sine = np.cos(angles), -np.sin(angles)
    for x in range(count):
        for colour in range(3):
            re, im = row_at(x, colour, 0), row_at(x, colour, 1)
            swap[re, im], swap[im, re] = -1.0, 1.0
            spin[re, re], spin[re, im] = cosine[x], -sine[x]
            spin[im, im], spin[im, re] = cosine[x], sine[x]
    fixed = np.zeros((2, rows, 2, 128), BF16)
    fixed[0, :, 0, :rows] = swap.astype(BF16)
    fixed[1, :, 0, :rows], fixed[1, :, 1, :rows] = split(spin)
    spread = np.zeros((2, 128, 2, 128), np.float32)
    masks = np.zeros((2, rows, 128), np.float32)
    for shift in range(2):
        for x in range(count):
            there = (x + shift) % count
            for colour in range(3):
                for part in range(2):
                    for to_part in range(2):
                        lane = ((part ^ to_part) * 3 + colour) * count + x
                        sign = -1.0 if (part, to_part) == (0, 1) else 1.0
                        spread[shift, lane, part, row_at(there, colour, to_part)] = sign
            masks[shift, 6 * x : 6 * x + 6, 6 * there : 6 * there + 6] = 1.0
    return (
        fixed.reshape(2 * rows, 256),
        spread.reshape(2, 128, 256).astype(BF16),
        masks.astype(BF16),
    )


def site_rows(site, rows):
    return pl.ds(pl.multiple_of(site * rows, rows), rows)


def spread_links(flat, spread):
    high = flat.astype(jnp.bfloat16)
    low = (flat - high.astype(jnp.float32)).astype(jnp.bfloat16)
    return [jnp.dot(half, spread, preferred_element_type=jnp.float32) for half in (high, low)]


def store_coefs(coefs, base, stride, wide, sites):
    for colour in range(3):
        for part in range(2):
            for half in range(2):
                value = wide[half][colour * sites : (colour + 1) * sites, part * 128 : part * 128 + 128]
                for copy in range(4):
                    first = base + half * stride + copy * 6 + colour * 2 + part
                    coefs[pl.ds(first, sites, stride=24), :] = value


def block_matrix(coefs, start, stride, rows, mask):
    halves = []
    for half in range(2):
        value = coefs[pl.ds(pl.multiple_of(start + half * stride, 24), 24), :]
        value = jnp.concatenate([value, value], axis=0).astype(jnp.bfloat16)
        halves.append(jnp.concatenate([value] * (rows // 48), axis=0) * mask)
    return jnp.concatenate(halves, axis=1)


def apply(matrices, source):
    rows, width = source.shape
    padding = jnp.zeros((128 - rows, width), source.dtype)
    return jnp.dot(
        jnp.concatenate(matrices, axis=0),
        jnp.concatenate([source, padding, source, padding], axis=0),
        preferred_element_type=jnp.float32,
    ).astype(jnp.bfloat16)


def make_face(links, spread, coefs, face, direction, first, number, chosen, count, mask, source):
    rows = 6 * count
    sites = links.shape[0] // 54
    flat = []
    for other in range(3):
        pieces = []
        for part in range(2):
            for colour in range(3):
                start = (((direction * 2 + part) * 3 + colour) * 3 + other) * sites
                piece = links[pl.ds(start + first, number), :]
                pieces.append(-piece if part else piece)
        pieces.append(jnp.zeros((number, 128 - rows), jnp.float32))
        flat.append(jnp.concatenate(pieces, axis=1))
    wide = spread_links(jnp.concatenate(flat, axis=0), spread[0])
    store_coefs(coefs, 0, number * 24, wide, number)
    mask, source = mask(), source()
    for i, site in enumerate(chosen):
        matrix = block_matrix(coefs, (site - first) * 24, number * 24, rows, mask)
        face[site_rows(i, rows), :] = apply([matrix], source[site_rows(site, rows), :])


def first_kernel(
    slab_y, slab_z, count, v_hbm, links_hbm, fixed_hbm, spread_hbm, masks_hbm,
    face_y, face_z, v_ref, links, fixed, spread, masks, coefs, sems,
):
    sites = slab_y * slab_z
    parts = [pl.ds(i * 18 * sites, 18 * sites) for i in range(3)]
    pairs = [
        (links_hbm.at[parts[1]], links.at[parts[1]]),
        (spread_hbm, spread),
        (masks_hbm, masks),
        (v_hbm, v_ref),
        (links_hbm.at[parts[2]], links.at[parts[2]]),
        (links_hbm.at[parts[0]], links.at[parts[0]]),
        (fixed_hbm, fixed),
    ]
    moves = [pltpu.make_async_copy(*pair, sems.at[i]) for i, pair in enumerate(pairs)]
    for move in moves:
        move.start()
    for move in moves[:2]:
        move.wait()

    def mask():
        moves[2].wait()
        return masks[0]

    def source():
        moves[3].wait()
        return v_ref

    chosen = range(sites - slab_z, sites)
    make_face(links, spread, coefs, face_y, 1, sites - 8, 8, chosen, count, mask, source)
    moves[4].wait()
    chosen = range(slab_z - 1, sites, slab_z)
    make_face(links, spread, coefs, face_z, 2, 0, sites, chosen, count, lambda: masks[0], lambda: v_ref)
    for move in moves[5:]:
        move.wait()


def local_kernel(
    slab_y, slab_z, count, v_ref, links, fixed, spread, masks, total, first_y, first_z,
    coefs, left, right,
):
    rows = 6 * count
    sites = slab_y * slab_z
    width = v_ref.shape[1]

    for direction in range(3):
        flat = []
        for colour in range(3):
            pieces = []
            for part in range(2):
                for other in range(3):
                    start = (((direction * 2 + part) * 3 + colour) * 3 + other) * sites
                    pieces.append(links[pl.ds(start, sites), :])
            pieces.append(jnp.zeros((sites, 128 - rows), jnp.float32))
            flat.append(jnp.concatenate(pieces, axis=1))
        wide = spread_links(jnp.concatenate(flat, axis=0), spread[1 if direction == 0 else 0])
        store_coefs(coefs, direction * sites * 24, 3 * sites * 24, wide, sites)

    def matrix(direction, site):
        start = (direction * sites + site) * 24
        return block_matrix(coefs, start, 3 * sites * 24, rows, masks[1 if direction == 0 else 0])

    def at(site):
        return site_rows(site, rows)

    def stack(source):
        padding = jnp.zeros((128 - rows, width), source.dtype)
        return jnp.concatenate([source, padding, source, padding], axis=0)

    def put(site, operator, image):
        high = image.astype(jnp.bfloat16)
        right[at(site), operator * width : (operator + 1) * width] = high
        right[at(site), (operator + 3) * width : (operator + 4) * width] = (image - high.astype(jnp.float32)).astype(jnp.bfloat16)

    for y in range(slab_y):
        for z in range(0, slab_z, 2):
            site = y * slab_z + z
            plans = []
            for here in (site, site + 1):
                plan = [(1, here, 0, here)]
                if y > 0:
                    plan.append((2, here - slab_z, 1, here - slab_z))
                if here > y * slab_z:
                    plan.append((3, here - 1, 2, here - 1))
                plans.append(plan)
            matrices = [[matrix(d, s) for _, _, d, s in plan] for plan in plans]
            columns = [stack(v_ref[at(site), :]), stack(v_ref[at(site + 1), :])]
            shared = jnp.dot(fixed[...], jnp.concatenate(columns, axis=1), preferred_element_type=jnp.float32)
            parts = [jnp.dot(jnp.concatenate(matrices[i], axis=0), columns[i], preferred_element_type=jnp.float32) for i in range(2)]
            for i, here in enumerate((site, site + 1)):
                left[at(here), :width] = v_ref[at(here), :]
                mine = shared[:, i * width : (i + 1) * width].astype(jnp.bfloat16)
                left[at(here), width:] = mine[:rows]
                right[at(here), :width] = mine[rows:]
                for j, (operator, target, _, _) in enumerate(plans[i]):
                    put(target, operator, parts[i][j * rows : (j + 1) * rows])
        first_z[at(y), :] = left[at(y * slab_z), :]
        right[at(y * slab_z + slab_z - 1), 3 * width : 4 * width] = jnp.zeros((rows, width), jnp.bfloat16)
        right[at(y * slab_z + slab_z - 1), 6 * width : 7 * width] = jnp.zeros((rows, width), jnp.bfloat16)
    first_y[...] = left[pl.ds(0, slab_z * rows), :]
    last = pl.ds((slab_y - 1) * slab_z * rows, slab_z * rows)
    right[last, 2 * width : 3 * width] = jnp.zeros((slab_z * rows, width), jnp.bfloat16)
    right[last, 5 * width : 6 * width] = jnp.zeros((slab_z * rows, width), jnp.bfloat16)
    both = lax.dot_general(
        left[...], right[...], (((0,), (0,)), ((), ())), preferred_element_type=jnp.float32
    )
    total[:, :width] = both[:, :width]
    total[:, width:] = both[:, width : 4 * width] + both[:, 4 * width :]


def edge_kernel(scale, face_z, face_y, total, first_y, first_z, out, sums):
    width = face_y.shape[1]

    def product(first, face):
        return lax.dot_general(
            first[...], face[...], (((0,), (0,)), ((), ())), preferred_element_type=jnp.float32
        )

    extra = {2: product(first_y, face_y), 3: product(first_z, face_z)}
    for operator in range(4):
        both = total[:, operator * width : (operator + 1) * width]
        if operator in extra:
            both = both - extra[operator]
        real, imag = both[:width], both[width:]
        if operator == 0:
            real, imag = real * scale, imag * scale
        else:
            real, imag = (real - real.T) * (0.5 * scale), (imag + imag.T) * (0.5 * scale)
        sums[pl.ds(2 * operator, width, stride=8), :] = real
        sums[pl.ds(2 * operator + 1, width, stride=8), :] = imag
    out[...] = sums[...].astype(jnp.bfloat16)


def shifted(block, axis):
    size = lax.axis_size(axis)
    return lax.ppermute(block, axis, [(i, (i + 1) % size) for i in range(size)])


def per_device(eigenvectors, gauge_links):
    _, slab_y, slab_z, count, _, _, width = eigenvectors.shape
    rows = 6 * count
    sites = slab_y * slab_z
    scale = (6.0 * count * slab_y * lax.axis_size("gy") * slab_z * lax.axis_size("gz")) ** (-0.5)
    field = jnp.transpose(eigenvectors[0], (0, 1, 2, 4, 3, 5)).reshape(sites * rows, width)
    links = gauge_links.reshape(54 * sites, count)
    fixed, spread, masks = constants(count)
    inputs = (field, links, fixed, spread, masks)
    face_y, face_z, *inputs = pl.pallas_call(
        functools.partial(first_kernel, slab_y, slab_z, count),
        out_shape=[
            pltpu.VMEM((slab_z * rows, width), jnp.bfloat16),
            pltpu.VMEM((slab_y * rows, width), jnp.bfloat16),
            *(pltpu.VMEM(each.shape, each.dtype) for each in inputs),
        ],
        in_specs=[pl.BlockSpec(memory_space=pltpu.HBM)] * 5,
        scratch_shapes=[
            pltpu.VMEM((2 * sites * 24, 128), jnp.float32),
            pltpu.SemaphoreType.DMA((7,)),
        ],
        compiler_params=pltpu.CompilerParams(vmem_limit_bytes=24 * 1024 * 1024),
        cost_estimate=pl.CostEstimate(flops=2_000_000_000, bytes_accessed=600_000, transcendentals=0),
    )(*(pltpu.with_memory_space_constraint(each, pltpu.HBM) for each in inputs))
    face_y = shifted(face_y, "gy")
    face_z = shifted(face_z, "gz")
    total, first_y, first_z = pl.pallas_call(
        functools.partial(local_kernel, slab_y, slab_z, count),
        out_shape=[
            jax.ShapeDtypeStruct((2 * width, 4 * width), jnp.float32),
            jax.ShapeDtypeStruct((slab_z * rows, 2 * width), jnp.bfloat16),
            jax.ShapeDtypeStruct((slab_y * rows, 2 * width), jnp.bfloat16),
        ],
        scratch_shapes=[
            pltpu.VMEM((6 * sites * 24, 128), jnp.float32),
            pltpu.VMEM((sites * rows, 2 * width), jnp.bfloat16),
            pltpu.VMEM((sites * rows, 7 * width), jnp.bfloat16),
        ],
        compiler_params=pltpu.CompilerParams(vmem_limit_bytes=32 * 1024 * 1024),
        cost_estimate=pl.CostEstimate(flops=5_000_000_000, bytes_accessed=4_000_000, transcendentals=0),
    )(*inputs)
    partial = pl.pallas_call(
        functools.partial(edge_kernel, scale),
        out_shape=jax.ShapeDtypeStruct((8 * width, width), jnp.bfloat16),
        scratch_shapes=[pltpu.VMEM((8 * width, width), jnp.float32)],
        compiler_params=pltpu.CompilerParams(vmem_limit_bytes=16 * 1024 * 1024),
    )(face_z, face_y, total, first_y, first_z)
    gathered = lax.all_to_all(partial.reshape(width, 8, width), ("gy", "gz"), 0, 0, tiled=True)
    return jnp.sum(gathered.astype(jnp.float32), axis=0).reshape(1, 1, 4, 2, width)


def solution(mesh):
    placed = (
        P(None, "gy", "gz", None, None, None, None),
        P(None, None, None, None, None, "gy", "gz", None),
    )
    return jax.shard_map(
        per_device,
        mesh=mesh,
        in_specs=placed,
        out_specs=P(("gy", "gz"), None, None, None, None),
        check_vma=False,
    )
```

```python
import functools

import jax
import jax.numpy as jnp
import ml_dtypes
import numpy as np
from jax import lax
from jax.experimental import pallas as pl
from jax.experimental.pallas import tpu as pltpu
from jax.sharding import PartitionSpec as P

BF16 = ml_dtypes.bfloat16


def split(value):
    high = value.astype(BF16)
    low = (value - high.astype(np.float32)).astype(BF16)
    return high, low


def row_at(x, colour, part):
    return (x * 3 + colour) * 2 + part


def constants(count):
    rows = 6 * count
    swap = np.zeros((rows, rows), np.float32)
    spin = np.zeros((rows, rows), np.float32)
    angles = np.arange(count, dtype=np.float32) * np.float32(2.0 * np.pi / count)
    cosine, sine = np.cos(angles), -np.sin(angles)
    for x in range(count):
        for colour in range(3):
            re, im = row_at(x, colour, 0), row_at(x, colour, 1)
            swap[re, im], swap[im, re] = -1.0, 1.0
            spin[re, re], spin[re, im] = cosine[x], -sine[x]
            spin[im, im], spin[im, re] = cosine[x], sine[x]
    fixed = np.zeros((2, rows, 2, 128), BF16)
    fixed[0, :, 0, :rows] = swap.astype(BF16)
    fixed[1, :, 0, :rows], fixed[1, :, 1, :rows] = split(spin)
    spread = np.zeros((2, 128, 2, 128), np.float32)
    masks = np.zeros((2, rows, 128), np.float32)
    for shift in range(2):
        for x in range(count):
            there = (x + shift) % count
            for colour in range(3):
                for part in range(2):
                    for to_part in range(2):
                        lane = ((part ^ to_part) * 3 + colour) * count + x
                        sign = -1.0 if (part, to_part) == (0, 1) else 1.0
                        spread[shift, lane, part, row_at(there, colour, to_part)] = sign
            masks[shift, 6 * x : 6 * x + 6, 6 * there : 6 * there + 6] = 1.0
    return (
        fixed.reshape(2 * rows, 256),
        spread.reshape(2, 128, 256).astype(BF16),
        masks.astype(BF16),
    )


def site_rows(site, rows):
    return pl.ds(pl.multiple_of(site * rows, rows), rows)


def spread_links(flat, spread):
    high = flat.astype(jnp.bfloat16)
    low = (flat - high.astype(jnp.float32)).astype(jnp.bfloat16)
    return [jnp.dot(half, spread, preferred_element_type=jnp.float32) for half in (high, low)]


def store_coefs(coefs, base, stride, wide, sites):
    for colour in range(3):
        for part in range(2):
            for half in range(2):
                value = wide[half][colour * sites : (colour + 1) * sites, part * 128 : part * 128 + 128]
                for copy in range(4):
                    first = base + half * stride + copy * 6 + colour * 2 + part
                    coefs[pl.ds(first, sites, stride=24), :] = value


def block_matrix(coefs, start, stride, rows, mask):
    halves = []
    for half in range(2):
        value = coefs[pl.ds(pl.multiple_of(start + half * stride, 24), 24), :]
        value = jnp.concatenate([value, value], axis=0).astype(jnp.bfloat16)
        halves.append(jnp.concatenate([value] * (rows // 48), axis=0) * mask)
    return jnp.concatenate(halves, axis=1)


def apply(matrices, source):
    rows, width = source.shape
    padding = jnp.zeros((128 - rows, width), source.dtype)
    return jnp.dot(
        jnp.concatenate(matrices, axis=0),
        jnp.concatenate([source, padding, source, padding], axis=0),
        preferred_element_type=jnp.float32,
    ).astype(jnp.bfloat16)


def back_links(links, direction, first, number, count):
    flat = []
    for other in range(3):
        pieces = []
        for part in range(2):
            for colour in range(3):
                piece = links[((direction * 2 + part) * 3 + colour) * 3 + other, pl.ds(first, number), :]
                pieces.append(-piece if part else piece)
        pieces.append(jnp.zeros((number, 128 - 6 * count), jnp.float32))
        flat.append(jnp.concatenate(pieces, axis=1))
    return jnp.concatenate(flat, axis=0)


def first_kernel(
    slab_y, slab_z, count, v_hbm, links_hbm, fixed_hbm, spread_hbm, masks_hbm,
    face_y, face_z, v_ref, links, fixed, spread, masks, flat, coefs_y, coefs_z, sems,
):
    sites = slab_y * slab_z
    mine, others = pl.ds(0, slab_y - 1), pl.ds(0, slab_z - 1)
    along_x, along_y, along_z = (pl.ds(18 * i, 18) for i in range(3))
    whole = (slice(None),)
    pairs = [
        (links_hbm, links, (along_z,)),
        (spread_hbm, spread, whole),
        (links_hbm, links, (along_y, pl.ds(sites - 8, 8))),
        (masks_hbm, masks, whole),
        (v_hbm, v_ref, (slab_y - 1,)),
        (v_hbm, v_ref, (mine, slab_z - 1)),
        (links_hbm, links, (along_x,)),
        (links_hbm, links, (along_y, pl.ds(0, sites - 8))),
        (v_hbm, v_ref, (mine, others)),
        (fixed_hbm, fixed, whole),
    ]
    moves = [
        pltpu.make_async_copy(source.at[where], target.at[where], sems.at[i])
        for i, (source, target, where) in enumerate(pairs)
    ]
    for move in moves:
        move.start()
    rows = 6 * count
    for move in moves[:3]:
        move.wait()
    flat[...] = back_links(links, 2, 0, sites, count)
    edge = flat[pl.ds(slab_z - 1, 3 * slab_y, stride=slab_z), :]
    store_coefs(coefs_z, 0, slab_y * 24, spread_links(edge, spread[0]), slab_y)
    edge = back_links(links, 1, sites - 8, 8, count)
    store_coefs(coefs_y, 0, 8 * 24, spread_links(edge, spread[0]), 8)
    for move in moves[3:6]:
        move.wait()
    mask = masks[0]
    for z in range(slab_z):
        matrix = block_matrix(coefs_y, (8 - slab_z + z) * 24, 8 * 24, rows, mask)
        face_y[site_rows(z, rows), :] = apply([matrix], v_ref[slab_y - 1, z])
    for y in range(slab_y):
        matrix = block_matrix(coefs_z, y * 24, slab_y * 24, rows, mask)
        face_z[site_rows(y, rows), :] = apply([matrix], v_ref[y, slab_z - 1])
    for move in moves[6:]:
        move.wait()


def local_kernel(
    slab_y, slab_z, count, v_ref, links, fixed, spread, masks, total, first_y, first_z,
    coefs, left, right,
):
    rows = 6 * count
    sites = slab_y * slab_z
    width = v_ref.shape[-1]

    for direction in range(3):
        flat = []
        for colour in range(3):
            pieces = []
            for part in range(2):
                for other in range(3):
                    pieces.append(links[((direction * 2 + part) * 3 + colour) * 3 + other])
            pieces.append(jnp.zeros((sites, 128 - rows), jnp.float32))
            flat.append(jnp.concatenate(pieces, axis=1))
        wide = spread_links(jnp.concatenate(flat, axis=0), spread[1 if direction == 0 else 0])
        store_coefs(coefs, direction * sites * 24, 3 * sites * 24, wide, sites)

    def matrix(direction, site):
        start = (direction * sites + site) * 24
        return block_matrix(coefs, start, 3 * sites * 24, rows, masks[1 if direction == 0 else 0])

    def at(site):
        return site_rows(site, rows)

    def stack(source):
        padding = jnp.zeros((128 - rows, width), source.dtype)
        return jnp.concatenate([source, padding, source, padding], axis=0)

    def put(site, operator, image):
        high = image.astype(jnp.bfloat16)
        right[at(site), operator * width : (operator + 1) * width] = high
        right[at(site), (operator + 3) * width : (operator + 4) * width] = (image - high.astype(jnp.float32)).astype(jnp.bfloat16)

    for y in range(slab_y):
        for z in range(0, slab_z, 2):
            site = y * slab_z + z
            plans = []
            for here in (site, site + 1):
                plan = [(1, here, 0, here)]
                if y > 0:
                    plan.append((2, here - slab_z, 1, here - slab_z))
                if here > y * slab_z:
                    plan.append((3, here - 1, 2, here - 1))
                plans.append(plan)
            matrices = [[matrix(d, s) for _, _, d, s in plan] for plan in plans]
            columns = [stack(v_ref[y, z]), stack(v_ref[y, z + 1])]
            shared = jnp.dot(fixed[...], jnp.concatenate(columns, axis=1), preferred_element_type=jnp.float32)
            parts = [jnp.dot(jnp.concatenate(matrices[i], axis=0), columns[i], preferred_element_type=jnp.float32) for i in range(2)]
            for i, here in enumerate((site, site + 1)):
                left[at(here), :width] = v_ref[y, z + i]
                mine = shared[:, i * width : (i + 1) * width].astype(jnp.bfloat16)
                left[at(here), width:] = mine[:rows]
                right[at(here), :width] = mine[rows:]
                for j, (operator, target, _, _) in enumerate(plans[i]):
                    put(target, operator, parts[i][j * rows : (j + 1) * rows])
        first_z[at(y), :] = left[at(y * slab_z), :]
        right[at(y * slab_z + slab_z - 1), 3 * width : 4 * width] = jnp.zeros((rows, width), jnp.bfloat16)
        right[at(y * slab_z + slab_z - 1), 6 * width : 7 * width] = jnp.zeros((rows, width), jnp.bfloat16)
    first_y[...] = left[pl.ds(0, slab_z * rows), :]
    last = pl.ds((slab_y - 1) * slab_z * rows, slab_z * rows)
    right[last, 2 * width : 3 * width] = jnp.zeros((slab_z * rows, width), jnp.bfloat16)
    right[last, 5 * width : 6 * width] = jnp.zeros((slab_z * rows, width), jnp.bfloat16)
    both = lax.dot_general(
        left[...], right[...], (((0,), (0,)), ((), ())), preferred_element_type=jnp.float32
    )
    total[:, :width] = both[:, :width]
    total[:, width:] = both[:, width : 4 * width] + both[:, 4 * width :]


def edge_kernel(scale, face_z, face_y, total, first_y, first_z, out, sums):
    width = face_y.shape[1]

    def product(first, face):
        return lax.dot_general(
            first[...], face[...], (((0,), (0,)), ((), ())), preferred_element_type=jnp.float32
        )

    extra = {2: product(first_y, face_y), 3: product(first_z, face_z)}
    for operator in range(4):
        both = total[:, operator * width : (operator + 1) * width]
        if operator in extra:
            both = both - extra[operator]
        real, imag = both[:width], both[width:]
        if operator == 0:
            real, imag = real * scale, imag * scale
        else:
            real, imag = (real - real.T) * (0.5 * scale), (imag + imag.T) * (0.5 * scale)
        sums[pl.ds(2 * operator, width, stride=8), :] = real
        sums[pl.ds(2 * operator + 1, width, stride=8), :] = imag
    out[...] = sums[...].astype(jnp.bfloat16)


def shifted(block, axis):
    size = lax.axis_size(axis)
    return lax.ppermute(block, axis, [(i, (i + 1) % size) for i in range(size)])


def per_device(eigenvectors, gauge_links):
    _, slab_y, slab_z, count, _, _, width = eigenvectors.shape
    rows = 6 * count
    sites = slab_y * slab_z
    scale = (6.0 * count * slab_y * lax.axis_size("gy") * slab_z * lax.axis_size("gz")) ** (-0.5)
    field = jnp.transpose(eigenvectors[0], (0, 1, 2, 4, 3, 5)).reshape(slab_y, slab_z, rows, width)
    links = gauge_links.reshape(54, sites, count)
    fixed, spread, masks = constants(count)
    inputs = (field, links, fixed, spread, masks)
    face_y, face_z, *inputs = pl.pallas_call(
        functools.partial(first_kernel, slab_y, slab_z, count),
        out_shape=[
            pltpu.VMEM((slab_z * rows, width), jnp.bfloat16),
            pltpu.VMEM((slab_y * rows, width), jnp.bfloat16),
            *(pltpu.VMEM(each.shape, each.dtype) for each in inputs),
        ],
        in_specs=[pl.BlockSpec(memory_space=pltpu.HBM)] * 5,
        scratch_shapes=[
            pltpu.VMEM((3 * sites, 128), jnp.float32),
            pltpu.VMEM((2 * 8 * 24, 128), jnp.float32),
            pltpu.VMEM((2 * slab_y * 24, 128), jnp.float32),
            pltpu.SemaphoreType.DMA((10,)),
        ],
        compiler_params=pltpu.CompilerParams(vmem_limit_bytes=24 * 1024 * 1024),
        cost_estimate=pl.CostEstimate(flops=2_000_000_000, bytes_accessed=600_000, transcendentals=0),
    )(*(pltpu.with_memory_space_constraint(each, pltpu.HBM) for each in inputs))
    face_y = shifted(face_y, "gy")
    face_z = shifted(face_z, "gz")
    total, first_y, first_z = pl.pallas_call(
        functools.partial(local_kernel, slab_y, slab_z, count),
        out_shape=[
            jax.ShapeDtypeStruct((2 * width, 4 * width), jnp.float32),
            jax.ShapeDtypeStruct((slab_z * rows, 2 * width), jnp.bfloat16),
            jax.ShapeDtypeStruct((slab_y * rows, 2 * width), jnp.bfloat16),
        ],
        scratch_shapes=[
            pltpu.VMEM((6 * sites * 24, 128), jnp.float32),
            pltpu.VMEM((sites * rows, 2 * width), jnp.bfloat16),
            pltpu.VMEM((sites * rows, 7 * width), jnp.bfloat16),
        ],
        compiler_params=pltpu.CompilerParams(vmem_limit_bytes=32 * 1024 * 1024),
        cost_estimate=pl.CostEstimate(flops=5_000_000_000, bytes_accessed=4_000_000, transcendentals=0),
    )(*inputs)
    partial = pl.pallas_call(
        functools.partial(edge_kernel, scale),
        out_shape=jax.ShapeDtypeStruct((8 * width, width), jnp.bfloat16),
        scratch_shapes=[pltpu.VMEM((8 * width, width), jnp.float32)],
        compiler_params=pltpu.CompilerParams(vmem_limit_bytes=16 * 1024 * 1024),
    )(face_z, face_y, total, first_y, first_z)
    gathered = lax.all_to_all(partial.reshape(width, 8, width), ("gy", "gz"), 0, 0, tiled=True)
    return jnp.sum(gathered.astype(jnp.float32), axis=0).reshape(1, 1, 4, 2, width)


def solution(mesh):
    placed = (
        P(None, "gy", "gz", None, None, None, None),
        P(None, None, None, None, None, "gy", "gz", None),
    )
    return jax.shard_map(
        per_device,
        mesh=mesh,
        in_specs=placed,
        out_specs=P(("gy", "gz"), None, None, None, None),
        check_vma=False,
    )
```

```python
import functools

import jax
import jax.numpy as jnp
import ml_dtypes
import numpy as np
from jax import lax
from jax.experimental import pallas as pl
from jax.experimental.pallas import tpu as pltpu
from jax.sharding import PartitionSpec as P

BF16 = ml_dtypes.bfloat16


def row_at(x, colour, part):
    return (x * 3 + colour) * 2 + part


def constants(count):
    rows = 6 * count
    angles = np.arange(count, dtype=np.float32) * np.float32(2.0 * np.pi / count)
    waves = np.repeat(np.stack([np.cos(angles), -np.sin(angles)]), 6, axis=1)
    waves = np.broadcast_to(waves[..., None], (2, rows, 128)).astype(np.float32)
    spread = np.zeros((2, 128, 2, 128), np.float32)
    masks = np.zeros((3, rows, 128), np.float32)
    for shift in range(2):
        for x in range(count):
            there = (x + shift) % count
            for colour in range(3):
                for part in range(2):
                    for to_part in range(2):
                        lane = ((part ^ to_part) * 3 + colour) * count + x
                        sign = -1.0 if (part, to_part) == (0, 1) else 1.0
                        spread[shift, lane, part, row_at(there, colour, to_part)] = sign
            masks[shift, 6 * x : 6 * x + 6, 6 * there : 6 * there + 6] = 1.0
            if shift == 1:
                masks[2, 6 * there : 6 * there + 6, 6 * x : 6 * x + 6] = -1.0
    return (
        waves,
        spread.reshape(2, 128, 256).astype(BF16),
        masks.astype(BF16),
    )


def site_rows(site, rows):
    return pl.ds(pl.multiple_of(site * rows, rows), rows)


def spread_links(flat, spread):
    high = flat.astype(jnp.bfloat16)
    low = (flat - high.astype(jnp.float32)).astype(jnp.bfloat16)
    return [jnp.dot(half, spread, preferred_element_type=jnp.float32) for half in (high, low)]


def store_coefs(coefs, base, stride, wide, sites):
    for colour in range(3):
        for part in range(2):
            for half in range(2):
                value = wide[half][colour * sites : (colour + 1) * sites, part * 128 : part * 128 + 128]
                for copy in range(4):
                    first = base + half * stride + copy * 6 + colour * 2 + part
                    coefs[pl.ds(first, sites, stride=24), :] = value


def block_matrix(coefs, start, stride, rows, mask):
    halves = []
    for half in range(2):
        value = coefs[pl.ds(pl.multiple_of(start + half * stride, 24), 24), :]
        value = jnp.concatenate([value, value], axis=0).astype(jnp.bfloat16)
        halves.append(jnp.concatenate([value] * (rows // 48), axis=0) * mask)
    return jnp.concatenate(halves, axis=1)


def apply(matrices, source):
    rows, width = source.shape
    padding = jnp.zeros((128 - rows, width), source.dtype)
    return jnp.dot(
        jnp.concatenate(matrices, axis=0),
        jnp.concatenate([source, padding, source, padding], axis=0),
        preferred_element_type=jnp.float32,
    ).astype(jnp.bfloat16)


def back_links(links, direction, first, number, count):
    flat = []
    for other in range(3):
        pieces = []
        for part in range(2):
            for colour in range(3):
                piece = links[((direction * 2 + part) * 3 + colour) * 3 + other, pl.ds(first, number), :]
                pieces.append(-piece if part else piece)
        pieces.append(jnp.zeros((number, 128 - 6 * count), jnp.float32))
        flat.append(jnp.concatenate(pieces, axis=1))
    return jnp.concatenate(flat, axis=0)


def first_kernel(
    slab_y, slab_z, count, v_hbm, links_hbm, waves_hbm, spread_hbm, masks_hbm,
    face_y, face_z, v_ref, links, waves, spread, masks, flat, coefs_y, coefs_z, sems,
):
    sites = slab_y * slab_z
    mine, others = pl.ds(0, slab_y - 1), pl.ds(0, slab_z - 1)
    along_x, along_y, along_z = (pl.ds(18 * i, 18) for i in range(3))
    whole = (slice(None),)
    pairs = [
        (links_hbm, links, (along_z,)),
        (spread_hbm, spread, whole),
        (links_hbm, links, (along_y, pl.ds(sites - 8, 8))),
        (masks_hbm, masks, whole),
        (v_hbm, v_ref, (slab_y - 1,)),
        (v_hbm, v_ref, (mine, slab_z - 1)),
        (links_hbm, links, (along_x,)),
        (links_hbm, links, (along_y, pl.ds(0, sites - 8))),
        (v_hbm, v_ref, (mine, others)),
        (waves_hbm, waves, whole),
    ]
    moves = [
        pltpu.make_async_copy(source.at[where], target.at[where], sems.at[i])
        for i, (source, target, where) in enumerate(pairs)
    ]
    for move in moves:
        move.start()
    rows = 6 * count
    for move in moves[:3]:
        move.wait()
    flat[...] = back_links(links, 2, 0, sites, count)
    edge = flat[pl.ds(slab_z - 1, 3 * slab_y, stride=slab_z), :]
    store_coefs(coefs_z, 0, slab_y * 24, spread_links(edge, spread[0]), slab_y)
    edge = back_links(links, 1, sites - 8, 8, count)
    store_coefs(coefs_y, 0, 8 * 24, spread_links(edge, spread[0]), 8)
    for move in moves[3:6]:
        move.wait()
    mask = masks[0]
    jobs = [(face_y, z, coefs_y, 8 - slab_z + z, v_ref[slab_y - 1, z]) for z in range(slab_z)]
    jobs += [(face_z, y, coefs_z, y, v_ref[y, slab_z - 1]) for y in range(slab_y)]
    for pair in zip(jobs[::2], jobs[1::2]):
        matrices = [block_matrix(table, at * 24, 8 * 24, rows, mask) for _, _, table, at, _ in pair]
        images = apply(matrices, jnp.concatenate([job[4] for job in pair], axis=1))
        for i, (face, at, *_) in enumerate(pair):
            width = face.shape[1]
            face[site_rows(at, rows), :] = images[i * rows : (i + 1) * rows, i * width : (i + 1) * width]
    for move in moves[6:]:
        move.wait()


def local_kernel(
    slab_y, slab_z, count, v_ref, links, waves, spread, masks, total, first_y, first_z,
    coefs, left, right,
):
    rows = 6 * count
    sites = slab_y * slab_z
    width = v_ref.shape[-1]

    for direction in range(3):
        flat = []
        for colour in range(3):
            pieces = []
            for part in range(2):
                for other in range(3):
                    pieces.append(links[((direction * 2 + part) * 3 + colour) * 3 + other])
            pieces.append(jnp.zeros((sites, 128 - rows), jnp.float32))
            flat.append(jnp.concatenate(pieces, axis=1))
        wide = spread_links(jnp.concatenate(flat, axis=0), spread[1 if direction == 0 else 0])
        store_coefs(coefs, direction * sites * 24, 4 * sites * 24, wide, sites)
    wide = spread_links(back_links(links, 0, 0, sites, count), spread[0])
    store_coefs(coefs, 3 * sites * 24, 4 * sites * 24, wide, sites)

    def matrix(direction, site):
        start, stride = (direction * sites + site) * 24, 4 * sites * 24
        if direction > 0:
            return block_matrix(coefs, start, stride, rows, masks[0])
        ahead = block_matrix(coefs, start, stride, rows, masks[1])
        return ahead + block_matrix(coefs, (3 * sites + site) * 24, stride, rows, masks[2])

    def at(site):
        return site_rows(site, rows)

    def stack(source):
        padding = jnp.zeros((128 - rows, width), source.dtype)
        return jnp.concatenate([source, padding, source, padding], axis=0)

    is_real = lax.broadcasted_iota(jnp.int32, (rows // 8, 8, width), 1) % 2 == 0

    def put(site, operator, image):
        high = image.astype(jnp.bfloat16)
        right[at(site), operator * width : (operator + 1) * width] = high
        if operator > 1:
            low = (image - high.astype(jnp.float32)).astype(jnp.bfloat16)
            right[at(site), (operator + 2) * width : (operator + 3) * width] = low

    for y in range(slab_y):
        for z in range(0, slab_z, 2):
            site = y * slab_z + z
            plans = []
            for here in (site, site + 1):
                plan = [(1, here, 0, here)]
                if y > 0:
                    plan.append((2, here - slab_z, 1, here - slab_z))
                if here > y * slab_z:
                    plan.append((3, here - 1, 2, here - 1))
                plans.append(plan)
            matrices = [[matrix(d, s) for _, _, d, s in plan] for plan in plans]
            for i, here in enumerate((site, site + 1)):
                source = v_ref[y, z + i]
                part = jnp.dot(
                    jnp.concatenate(matrices[i], axis=0), stack(source), preferred_element_type=jnp.float32
                )
                tiles = source.astype(jnp.float32).reshape(rows // 8, 8, width)
                below, above = pltpu.roll(tiles, 7, 1), pltpu.roll(tiles, 1, 1)
                swapped = jnp.where(is_real, -below, above).reshape(rows, width)
                image = waves[0] * source.astype(jnp.float32) + waves[1] * swapped
                left[at(here), :width] = source
                left[at(here), width:] = swapped.astype(jnp.bfloat16)
                right[at(here), :width] = image.astype(jnp.bfloat16)
                for j, (operator, target, _, _) in enumerate(plans[i]):
                    put(target, operator, part[j * rows : (j + 1) * rows])
        first_z[at(y), :] = left[at(y * slab_z), :]
        right[at(y * slab_z + slab_z - 1), 3 * width : 4 * width] = jnp.zeros((rows, width), jnp.bfloat16)
        right[at(y * slab_z + slab_z - 1), 5 * width : 6 * width] = jnp.zeros((rows, width), jnp.bfloat16)
    first_y[...] = left[pl.ds(0, slab_z * rows), :]
    last = pl.ds((slab_y - 1) * slab_z * rows, slab_z * rows)
    right[last, 2 * width : 3 * width] = jnp.zeros((slab_z * rows, width), jnp.bfloat16)
    right[last, 4 * width : 5 * width] = jnp.zeros((slab_z * rows, width), jnp.bfloat16)
    both = lax.dot_general(
        left[...], right[...], (((0,), (0,)), ((), ())), preferred_element_type=jnp.float32
    )
    total[:, : 2 * width] = both[:, : 2 * width]
    total[:, 2 * width :] = both[:, 2 * width : 4 * width] + both[:, 4 * width :]


def edge_kernel(scale, face_z, face_y, total, first_y, first_z, out, sums):
    width = face_y.shape[1]

    def product(first, face):
        return lax.dot_general(
            first[...], face[...], (((0,), (0,)), ((), ())), preferred_element_type=jnp.float32
        )

    extra = {2: product(first_y, face_y), 3: product(first_z, face_z)}
    for operator in range(4):
        both = total[:, operator * width : (operator + 1) * width]
        if operator in extra:
            both = both - extra[operator]
        real, imag = both[:width], both[width:]
        if operator < 2:
            factor = scale if operator == 0 else 0.5 * scale
            real, imag = real * factor, imag * factor
        else:
            real, imag = (real - real.T) * (0.5 * scale), (imag + imag.T) * (0.5 * scale)
        sums[pl.ds(2 * operator, width, stride=8), :] = real
        sums[pl.ds(2 * operator + 1, width, stride=8), :] = imag
    out[...] = sums[...].astype(jnp.bfloat16)


def shifted(block, axis):
    size = lax.axis_size(axis)
    return lax.ppermute(block, axis, [(i, (i + 1) % size) for i in range(size)])


def per_device(eigenvectors, gauge_links):
    _, slab_y, slab_z, count, _, _, width = eigenvectors.shape
    rows = 6 * count
    sites = slab_y * slab_z
    scale = (6.0 * count * slab_y * lax.axis_size("gy") * slab_z * lax.axis_size("gz")) ** (-0.5)
    field = jnp.transpose(eigenvectors[0], (0, 1, 2, 4, 3, 5)).reshape(slab_y, slab_z, rows, width)
    links = gauge_links.reshape(54, sites, count)
    waves, spread, masks = constants(count)
    inputs = (field, links, waves, spread, masks)
    face_y, face_z, *inputs = pl.pallas_call(
        functools.partial(first_kernel, slab_y, slab_z, count),
        out_shape=[
            pltpu.VMEM((slab_z * rows, width), jnp.bfloat16),
            pltpu.VMEM((slab_y * rows, width), jnp.bfloat16),
            *(pltpu.VMEM(each.shape, each.dtype) for each in inputs),
        ],
        in_specs=[pl.BlockSpec(memory_space=pltpu.HBM)] * 5,
        scratch_shapes=[
            pltpu.VMEM((3 * sites, 128), jnp.float32),
            pltpu.VMEM((2 * 8 * 24, 128), jnp.float32),
            pltpu.VMEM((2 * slab_y * 24, 128), jnp.float32),
            pltpu.SemaphoreType.DMA((10,)),
        ],
        compiler_params=pltpu.CompilerParams(vmem_limit_bytes=24 * 1024 * 1024),
        cost_estimate=pl.CostEstimate(flops=2_000_000_000, bytes_accessed=600_000, transcendentals=0),
    )(*(pltpu.with_memory_space_constraint(each, pltpu.HBM) for each in inputs))
    face_y = shifted(face_y, "gy")
    face_z = shifted(face_z, "gz")
    total, first_y, first_z = pl.pallas_call(
        functools.partial(local_kernel, slab_y, slab_z, count),
        out_shape=[
            jax.ShapeDtypeStruct((2 * width, 4 * width), jnp.float32),
            jax.ShapeDtypeStruct((slab_z * rows, 2 * width), jnp.bfloat16),
            jax.ShapeDtypeStruct((slab_y * rows, 2 * width), jnp.bfloat16),
        ],
        scratch_shapes=[
            pltpu.VMEM((8 * sites * 24, 128), jnp.float32),
            pltpu.VMEM((sites * rows, 2 * width), jnp.bfloat16),
            pltpu.VMEM((sites * rows, 6 * width), jnp.bfloat16),
        ],
        compiler_params=pltpu.CompilerParams(vmem_limit_bytes=32 * 1024 * 1024),
        cost_estimate=pl.CostEstimate(flops=5_000_000_000, bytes_accessed=4_000_000, transcendentals=0),
    )(*inputs)
    partial = pl.pallas_call(
        functools.partial(edge_kernel, scale),
        out_shape=jax.ShapeDtypeStruct((8 * width, width), jnp.bfloat16),
        scratch_shapes=[pltpu.VMEM((8 * width, width), jnp.float32)],
        compiler_params=pltpu.CompilerParams(vmem_limit_bytes=16 * 1024 * 1024),
    )(face_z, face_y, total, first_y, first_z)
    gathered = lax.all_to_all(partial.reshape(width, 8, width), ("gy", "gz"), 0, 0, tiled=True)
    return jnp.sum(gathered.astype(jnp.float32), axis=0).reshape(1, 1, 4, 2, width)


def solution(mesh):
    placed = (
        P(None, "gy", "gz", None, None, None, None),
        P(None, None, None, None, None, "gy", "gz", None),
    )
    return jax.shard_map(
        per_device,
        mesh=mesh,
        in_specs=placed,
        out_specs=P(("gy", "gz"), None, None, None, None),
        check_vma=False,
    )
```

```python
import functools

import jax
import jax.numpy as jnp
import ml_dtypes
import numpy as np
from jax import lax
from jax.experimental import pallas as pl
from jax.experimental.pallas import tpu as pltpu
from jax.sharding import PartitionSpec as P

BF16 = ml_dtypes.bfloat16


def row_at(x, colour, part):
    return (x * 3 + colour) * 2 + part


def constants(count):
    rows = 6 * count
    angles = np.arange(count, dtype=np.float32) * np.float32(2.0 * np.pi / count)
    waves = np.repeat(np.stack([np.cos(angles), -np.sin(angles)]), 6, axis=1)
    waves = np.broadcast_to(waves[..., None], (2, rows, 128)).astype(np.float32)
    spread = np.zeros((2, 128, 2, 128), np.float32)
    masks = np.zeros((3, rows, 128), np.float32)
    for shift in range(2):
        for x in range(count):
            there = (x + shift) % count
            for colour in range(3):
                for part in range(2):
                    for to_part in range(2):
                        lane = ((part ^ to_part) * 3 + colour) * count + x
                        sign = -1.0 if (part, to_part) == (0, 1) else 1.0
                        spread[shift, lane, part, row_at(there, colour, to_part)] = sign
            masks[shift, 6 * x : 6 * x + 6, 6 * there : 6 * there + 6] = 1.0
            if shift == 1:
                masks[2, 6 * there : 6 * there + 6, 6 * x : 6 * x + 6] = -1.0
    return (
        waves,
        spread.reshape(2, 128, 256).astype(BF16),
        masks.astype(BF16),
    )


def site_rows(site, rows):
    return pl.ds(pl.multiple_of(site * rows, rows), rows)


def spread_links(flat, spread):
    high = flat.astype(jnp.bfloat16)
    low = (flat - high.astype(jnp.float32)).astype(jnp.bfloat16)
    return [jnp.dot(half, spread, preferred_element_type=jnp.float32) for half in (high, low)]


def store_coefs(coefs, base, stride, wide, sites):
    for colour in range(3):
        for part in range(2):
            for half in range(2):
                value = wide[half][colour * sites : (colour + 1) * sites, part * 128 : part * 128 + 128]
                for copy in range(4):
                    first = base + half * stride + copy * 6 + colour * 2 + part
                    coefs[pl.ds(first, sites, stride=24), :] = value


def block_matrix(coefs, start, stride, rows, mask):
    halves = []
    for half in range(2):
        value = coefs[pl.ds(pl.multiple_of(start + half * stride, 24), 24), :]
        value = jnp.concatenate([value, value], axis=0).astype(jnp.bfloat16)
        halves.append(jnp.concatenate([value] * (rows // 48), axis=0) * mask)
    return jnp.concatenate(halves, axis=1)


def apply(matrices, source):
    rows, width = source.shape
    padding = jnp.zeros((128 - rows, width), source.dtype)
    return jnp.dot(
        jnp.concatenate(matrices, axis=0),
        jnp.concatenate([source, padding, source, padding], axis=0),
        preferred_element_type=jnp.float32,
    ).astype(jnp.bfloat16)


def back_links(links, direction, first, number, count):
    flat = []
    for other in range(3):
        pieces = []
        for part in range(2):
            for colour in range(3):
                piece = links[((direction * 2 + part) * 3 + colour) * 3 + other, pl.ds(first, number), :]
                pieces.append(-piece if part else piece)
        pieces.append(jnp.zeros((number, 128 - 6 * count), jnp.float32))
        flat.append(jnp.concatenate(pieces, axis=1))
    return jnp.concatenate(flat, axis=0)


def first_kernel(
    slab_y, slab_z, count, v_hbm, links_hbm, waves_hbm, spread_hbm, masks_hbm,
    face_y, face_z, v_ref, links, waves, spread, masks, flat, coefs_y, coefs_z, sems,
):
    sites = slab_y * slab_z
    mine, others = pl.ds(0, slab_y - 1), pl.ds(0, slab_z - 1)
    along_x, along_y, along_z = (pl.ds(18 * i, 18) for i in range(3))
    whole = (slice(None),)
    pairs = [
        (links_hbm, links, (along_z,)),
        (spread_hbm, spread, whole),
        (links_hbm, links, (along_y, pl.ds(sites - 8, 8))),
        (masks_hbm, masks, whole),
        (v_hbm, v_ref, (slab_y - 1,)),
        (v_hbm, v_ref, (mine, slab_z - 1)),
        (links_hbm, links, (along_x,)),
        (links_hbm, links, (along_y, pl.ds(0, sites - 8))),
        (v_hbm, v_ref, (mine, others)),
        (waves_hbm, waves, whole),
    ]
    moves = [
        pltpu.make_async_copy(source.at[where], target.at[where], sems.at[i])
        for i, (source, target, where) in enumerate(pairs)
    ]
    for move in moves:
        move.start()
    rows = 6 * count
    for move in moves[:3]:
        move.wait()
    flat[...] = back_links(links, 2, 0, sites, count)
    edge = flat[pl.ds(slab_z - 1, 3 * slab_y, stride=slab_z), :]
    store_coefs(coefs_z, 0, slab_y * 24, spread_links(edge, spread[0]), slab_y)
    edge = back_links(links, 1, sites - 8, 8, count)
    store_coefs(coefs_y, 0, 8 * 24, spread_links(edge, spread[0]), 8)
    for move in moves[3:6]:
        move.wait()
    mask = masks[0]
    jobs = [(face_y, z, coefs_y, 8 - slab_z + z, v_ref[slab_y - 1, z]) for z in range(slab_z)]
    jobs += [(face_z, y, coefs_z, y, v_ref[y, slab_z - 1]) for y in range(slab_y)]
    for pair in zip(jobs[::2], jobs[1::2]):
        matrices = [block_matrix(table, at * 24, 8 * 24, rows, mask) for _, _, table, at, _ in pair]
        images = apply(matrices, jnp.concatenate([job[4] for job in pair], axis=1))
        for i, (face, at, *_) in enumerate(pair):
            width = face.shape[1]
            face[site_rows(at, rows), :] = images[i * rows : (i + 1) * rows, i * width : (i + 1) * width]
    for move in moves[6:]:
        move.wait()


def local_kernel(
    slab_y, slab_z, count, v_ref, links, waves, spread, masks, total, first_y, first_z,
    coefs, left, right,
):
    rows = 6 * count
    sites = slab_y * slab_z
    width = v_ref.shape[-1]

    for direction in range(3):
        flat = []
        for colour in range(3):
            pieces = []
            for part in range(2):
                for other in range(3):
                    pieces.append(links[((direction * 2 + part) * 3 + colour) * 3 + other])
            pieces.append(jnp.zeros((sites, 128 - rows), jnp.float32))
            flat.append(jnp.concatenate(pieces, axis=1))
        wide = spread_links(jnp.concatenate(flat, axis=0), spread[1 if direction == 0 else 0])
        store_coefs(coefs, direction * sites * 24, 4 * sites * 24, wide, sites)
    wide = spread_links(back_links(links, 0, 0, sites, count), spread[0])
    store_coefs(coefs, 3 * sites * 24, 4 * sites * 24, wide, sites)

    def matrix(direction, site):
        start, stride = (direction * sites + site) * 24, 4 * sites * 24
        if direction > 0:
            return block_matrix(coefs, start, stride, rows, masks[0])
        ahead = block_matrix(coefs, start, stride, rows, masks[1])
        return ahead + block_matrix(coefs, (3 * sites + site) * 24, stride, rows, masks[2])

    def at(site):
        return site_rows(site, rows)

    def stack(source):
        padding = jnp.zeros((128 - rows, width), source.dtype)
        return jnp.concatenate([source, padding, source, padding], axis=0)

    is_real = lax.broadcasted_iota(jnp.int32, (rows // 8, 8, width), 1) % 2 == 0

    def put(site, operator, image):
        high = image.astype(jnp.bfloat16)
        right[at(site), operator * width : (operator + 1) * width] = high
        if operator > 1:
            low = (image - high.astype(jnp.float32)).astype(jnp.bfloat16)
            right[at(site), (operator + 2) * width : (operator + 3) * width] = low

    for y in range(slab_y):
        for z in range(0, slab_z, 2):
            site = y * slab_z + z
            plans = []
            for here in (site, site + 1):
                plan = [(1, here, 0, here)]
                if y > 0:
                    plan.append((2, here - slab_z, 1, here - slab_z))
                if here > y * slab_z:
                    plan.append((3, here - 1, 2, here - 1))
                plans.append(plan)
            matrices = [[matrix(d, s) for _, _, d, s in plan] for plan in plans]
            for i, here in enumerate((site, site + 1)):
                source = v_ref[y, z + i]
                part = jnp.dot(
                    jnp.concatenate(matrices[i], axis=0), stack(source), preferred_element_type=jnp.float32
                )
                tiles = source.astype(jnp.float32).reshape(rows // 8, 8, width)
                below, above = pltpu.roll(tiles, 7, 1), pltpu.roll(tiles, 1, 1)
                swapped = jnp.where(is_real, -below, above).reshape(rows, width)
                image = waves[0] * source.astype(jnp.float32) + waves[1] * swapped
                left[at(here), :width] = source
                left[at(here), width:] = swapped.astype(jnp.bfloat16)
                right[at(here), :width] = image.astype(jnp.bfloat16)
                for j, (operator, target, _, _) in enumerate(plans[i]):
                    put(target, operator, part[j * rows : (j + 1) * rows])
        first_z[at(y), :] = left[at(y * slab_z), :]
        right[at(y * slab_z + slab_z - 1), 3 * width : 4 * width] = jnp.zeros((rows, width), jnp.bfloat16)
        right[at(y * slab_z + slab_z - 1), 5 * width : 6 * width] = jnp.zeros((rows, width), jnp.bfloat16)
    first_y[...] = left[pl.ds(0, slab_z * rows), :]
    last = pl.ds((slab_y - 1) * slab_z * rows, slab_z * rows)
    right[last, 2 * width : 3 * width] = jnp.zeros((slab_z * rows, width), jnp.bfloat16)
    right[last, 4 * width : 5 * width] = jnp.zeros((slab_z * rows, width), jnp.bfloat16)
    both = lax.dot_general(
        left[...], right[...], (((0,), (0,)), ((), ())), preferred_element_type=jnp.float32
    )
    total[:, : 2 * width] = both[:, : 2 * width]
    total[:, 2 * width :] = both[:, 2 * width : 4 * width] + both[:, 4 * width :]


def edge_kernel(scale, face_z, face_y, total, first_y, first_z, out, sums):
    width = face_y.shape[1]

    def product(first, face):
        return lax.dot_general(
            first[...], face[...], (((0,), (0,)), ((), ())), preferred_element_type=jnp.float32
        )

    extra = {2: product(first_y, face_y), 3: product(first_z, face_z)}
    for operator in range(4):
        both = total[:, operator * width : (operator + 1) * width]
        if operator in extra:
            both = both - extra[operator]
        real, imag = both[:width], both[width:]
        if operator < 2:
            factor = scale if operator == 0 else 0.5 * scale
            real, imag = real * factor, imag * factor
        else:
            real, imag = (real - real.T) * (0.5 * scale), (imag + imag.T) * (0.5 * scale)
        sums[pl.ds(2 * operator, width, stride=8), :] = real
        sums[pl.ds(2 * operator + 1, width, stride=8), :] = imag
    out[...] = sums[...].astype(jnp.bfloat16)


def sum_kernel(gathered, out):
    pairs = gathered.shape[0] // 16
    sums = [jnp.zeros((16, gathered.shape[1]), jnp.float32) for _ in range(4)]
    for i in range(pairs):
        sums[i % 4] = sums[i % 4] + gathered[pl.ds(16 * i, 16), :].astype(jnp.float32)
    both = (sums[0] + sums[1]) + (sums[2] + sums[3])
    out[...] = both[:8] + both[8:]


def shifted(block, axis):
    size = lax.axis_size(axis)
    return lax.ppermute(block, axis, [(i, (i + 1) % size) for i in range(size)])


def per_device(eigenvectors, gauge_links):
    _, slab_y, slab_z, count, _, _, width = eigenvectors.shape
    rows = 6 * count
    sites = slab_y * slab_z
    scale = (6.0 * count * slab_y * lax.axis_size("gy") * slab_z * lax.axis_size("gz")) ** (-0.5)
    field = jnp.transpose(eigenvectors[0], (0, 1, 2, 4, 3, 5)).reshape(slab_y, slab_z, rows, width)
    links = gauge_links.reshape(54, sites, count)
    waves, spread, masks = constants(count)
    inputs = (field, links, waves, spread, masks)
    face_y, face_z, *inputs = pl.pallas_call(
        functools.partial(first_kernel, slab_y, slab_z, count),
        out_shape=[
            pltpu.VMEM((slab_z * rows, width), jnp.bfloat16),
            pltpu.VMEM((slab_y * rows, width), jnp.bfloat16),
            *(pltpu.VMEM(each.shape, each.dtype) for each in inputs),
        ],
        in_specs=[pl.BlockSpec(memory_space=pltpu.HBM)] * 5,
        scratch_shapes=[
            pltpu.VMEM((3 * sites, 128), jnp.float32),
            pltpu.VMEM((2 * 8 * 24, 128), jnp.float32),
            pltpu.VMEM((2 * slab_y * 24, 128), jnp.float32),
            pltpu.SemaphoreType.DMA((10,)),
        ],
        compiler_params=pltpu.CompilerParams(vmem_limit_bytes=24 * 1024 * 1024),
        cost_estimate=pl.CostEstimate(flops=2_000_000_000, bytes_accessed=600_000, transcendentals=0),
    )(*(pltpu.with_memory_space_constraint(each, pltpu.HBM) for each in inputs))
    face_y = shifted(face_y, "gy")
    face_z = shifted(face_z, "gz")
    total, first_y, first_z = pl.pallas_call(
        functools.partial(local_kernel, slab_y, slab_z, count),
        out_shape=[
            jax.ShapeDtypeStruct((2 * width, 4 * width), jnp.float32),
            jax.ShapeDtypeStruct((slab_z * rows, 2 * width), jnp.bfloat16),
            jax.ShapeDtypeStruct((slab_y * rows, 2 * width), jnp.bfloat16),
        ],
        scratch_shapes=[
            pltpu.VMEM((8 * sites * 24, 128), jnp.float32),
            pltpu.VMEM((sites * rows, 2 * width), jnp.bfloat16),
            pltpu.VMEM((sites * rows, 6 * width), jnp.bfloat16),
        ],
        compiler_params=pltpu.CompilerParams(vmem_limit_bytes=32 * 1024 * 1024),
        cost_estimate=pl.CostEstimate(flops=5_000_000_000, bytes_accessed=4_000_000, transcendentals=0),
    )(*inputs)
    partial = pl.pallas_call(
        functools.partial(edge_kernel, scale),
        out_shape=jax.ShapeDtypeStruct((8 * width, width), jnp.bfloat16),
        scratch_shapes=[pltpu.VMEM((8 * width, width), jnp.float32)],
        compiler_params=pltpu.CompilerParams(vmem_limit_bytes=16 * 1024 * 1024),
    )(face_z, face_y, total, first_y, first_z)
    gathered = lax.all_to_all(partial.reshape(width, 8, width), ("gy", "gz"), 0, 0, tiled=True)
    mine = pl.pallas_call(
        sum_kernel,
        out_shape=jax.ShapeDtypeStruct((8, width), jnp.float32),
        compiler_params=pltpu.CompilerParams(vmem_limit_bytes=8 * 1024 * 1024),
    )(gathered.reshape(8 * width, width))
    return mine.reshape(1, 1, 4, 2, width)


def solution(mesh):
    placed = (
        P(None, "gy", "gz", None, None, None, None),
        P(None, None, None, None, None, "gy", "gz", None),
    )
    return jax.shard_map(
        per_device,
        mesh=mesh,
        in_specs=placed,
        out_specs=P(("gy", "gz"), None, None, None, None),
        check_vma=False,
    )
```

```python
import functools

import jax
import jax.numpy as jnp
import ml_dtypes
import numpy as np
from jax import lax
from jax.experimental import pallas as pl
from jax.experimental.pallas import tpu as pltpu
from jax.sharding import PartitionSpec as P

BF16 = ml_dtypes.bfloat16


def row_at(x, colour, part):
    return (x * 3 + colour) * 2 + part


def constants(count):
    rows = 6 * count
    angles = np.arange(count, dtype=np.float32) * np.float32(2.0 * np.pi / count)
    waves = np.repeat(np.stack([np.cos(angles), -np.sin(angles)]), 6, axis=1)
    waves = np.broadcast_to(waves[..., None], (2, rows, 128)).astype(np.float32)
    spread = np.zeros((2, 128, 2, 128), np.float32)
    masks = np.zeros((3, rows, 128), np.float32)
    for shift in range(2):
        for x in range(count):
            there = (x + shift) % count
            for colour in range(3):
                for part in range(2):
                    for to_part in range(2):
                        lane = ((part ^ to_part) * 3 + colour) * count + x
                        sign = -1.0 if (part, to_part) == (0, 1) else 1.0
                        spread[shift, lane, part, row_at(there, colour, to_part)] = sign
            masks[shift, 6 * x : 6 * x + 6, 6 * there : 6 * there + 6] = 1.0
            if shift == 1:
                masks[2, 6 * there : 6 * there + 6, 6 * x : 6 * x + 6] = -1.0
    return (
        waves,
        spread.reshape(2, 128, 256).astype(BF16),
        masks.astype(BF16),
    )


def site_rows(site, rows):
    return pl.ds(pl.multiple_of(site * rows, rows), rows)


def spread_links(flat, spread):
    high = flat.astype(jnp.bfloat16)
    low = (flat - high.astype(jnp.float32)).astype(jnp.bfloat16)
    return [jnp.dot(half, spread, preferred_element_type=jnp.float32) for half in (high, low)]


def store_coefs(coefs, base, stride, wide, sites):
    for colour in range(3):
        for part in range(2):
            for half in range(2):
                value = wide[half][colour * sites : (colour + 1) * sites, part * 128 : part * 128 + 128]
                for copy in range(4):
                    first = base + half * stride + copy * 6 + colour * 2 + part
                    coefs[pl.ds(first, sites, stride=24), :] = value


def block_matrix(coefs, start, stride, rows, mask):
    halves = []
    for half in range(2):
        value = coefs[pl.ds(pl.multiple_of(start + half * stride, 24), 24), :]
        value = jnp.concatenate([value, value], axis=0).astype(jnp.bfloat16)
        halves.append(jnp.concatenate([value] * (rows // 48), axis=0) * mask)
    return jnp.concatenate(halves, axis=1)


def apply(matrices, source):
    rows, width = source.shape
    padding = jnp.zeros((128 - rows, width), source.dtype)
    return jnp.dot(
        jnp.concatenate(matrices, axis=0),
        jnp.concatenate([source, padding, source, padding], axis=0),
        preferred_element_type=jnp.float32,
    ).astype(jnp.bfloat16)


def back_links(links, direction, first, number, count):
    flat = []
    for other in range(3):
        pieces = []
        for part in range(2):
            for colour in range(3):
                piece = links[((direction * 2 + part) * 3 + colour) * 3 + other, pl.ds(first, number), :]
                pieces.append(-piece if part else piece)
        pieces.append(jnp.zeros((number, 128 - 6 * count), jnp.float32))
        flat.append(jnp.concatenate(pieces, axis=1))
    return jnp.concatenate(flat, axis=0)


def first_kernel(
    slab_y, slab_z, count, v_hbm, links_hbm, waves_hbm, spread_hbm, masks_hbm,
    face_y, face_z, v_ref, links, waves, spread, masks, flat, coefs_y, coefs_z, sems,
):
    sites = slab_y * slab_z
    mine, others = pl.ds(0, slab_y - 1), pl.ds(0, slab_z - 1)
    along_x, along_y, along_z = (pl.ds(18 * i, 18) for i in range(3))
    whole = (slice(None),)
    pairs = [
        (links_hbm, links, (along_z,)),
        (spread_hbm, spread, whole),
        (links_hbm, links, (along_y, pl.ds(sites - 8, 8))),
        (masks_hbm, masks, whole),
        (v_hbm, v_ref, (slab_y - 1,)),
        (v_hbm, v_ref, (mine, slab_z - 1)),
        (links_hbm, links, (along_x,)),
        (links_hbm, links, (along_y, pl.ds(0, sites - 8))),
        (v_hbm, v_ref, (mine, others)),
        (waves_hbm, waves, whole),
    ]
    moves = [
        pltpu.make_async_copy(source.at[where], target.at[where], sems.at[i])
        for i, (source, target, where) in enumerate(pairs)
    ]
    for move in moves:
        move.start()
    rows = 6 * count
    for move in moves[:3]:
        move.wait()
    flat[...] = back_links(links, 2, 0, sites, count)
    edge = flat[pl.ds(slab_z - 1, 3 * slab_y, stride=slab_z), :]
    store_coefs(coefs_z, 0, slab_y * 24, spread_links(edge, spread[0]), slab_y)
    edge = back_links(links, 1, sites - 8, 8, count)
    store_coefs(coefs_y, 0, 8 * 24, spread_links(edge, spread[0]), 8)
    for move in moves[3:6]:
        move.wait()
    mask = masks[0]
    jobs = [(face_y, z, coefs_y, 8 - slab_z + z, v_ref[slab_y - 1, z]) for z in range(slab_z)]
    jobs += [(face_z, y, coefs_z, y, v_ref[y, slab_z - 1]) for y in range(slab_y)]
    for pair in zip(jobs[::2], jobs[1::2]):
        matrices = [block_matrix(table, at * 24, 8 * 24, rows, mask) for _, _, table, at, _ in pair]
        images = apply(matrices, jnp.concatenate([job[4] for job in pair], axis=1))
        for i, (face, at, *_) in enumerate(pair):
            width = face.shape[1]
            face[site_rows(at, rows), :] = images[i * rows : (i + 1) * rows, i * width : (i + 1) * width]
    for move in moves[6:]:
        move.wait()


def local_kernel(
    slab_y, slab_z, count, v_ref, links, waves, spread, masks, total, turned, coefs, right
):
    rows = 6 * count
    sites = slab_y * slab_z
    width = v_ref.shape[-1]

    for direction in range(3):
        flat = []
        for colour in range(3):
            pieces = []
            for part in range(2):
                for other in range(3):
                    pieces.append(links[((direction * 2 + part) * 3 + colour) * 3 + other])
            pieces.append(jnp.zeros((sites, 128 - rows), jnp.float32))
            flat.append(jnp.concatenate(pieces, axis=1))
        wide = spread_links(jnp.concatenate(flat, axis=0), spread[1 if direction == 0 else 0])
        store_coefs(coefs, direction * sites * 24, 4 * sites * 24, wide, sites)
    wide = spread_links(back_links(links, 0, 0, sites, count), spread[0])
    store_coefs(coefs, 3 * sites * 24, 4 * sites * 24, wide, sites)

    mask = [masks[i] for i in range(3)]

    def matrix(direction, site):
        start, stride = (direction * sites + site) * 24, 4 * sites * 24
        if direction > 0:
            return block_matrix(coefs, start, stride, rows, mask[0])
        ahead = block_matrix(coefs, start, stride, rows, mask[1])
        return ahead + block_matrix(coefs, (3 * sites + site) * 24, stride, rows, mask[2])

    def at(site):
        return site_rows(site, rows)

    def stack(source):
        padding = jnp.zeros((128 - rows, width), source.dtype)
        return jnp.concatenate([source, padding, source, padding], axis=0)

    is_real = lax.broadcasted_iota(jnp.int32, (rows // 8, 8, width), 1) % 2 == 0

    def put(site, operator, image):
        high = image.astype(jnp.bfloat16)
        right[at(site), operator * width : (operator + 1) * width] = high
        if operator > 1:
            low = (image - high.astype(jnp.float32)).astype(jnp.bfloat16)
            right[at(site), (operator + 2) * width : (operator + 3) * width] = low

    for y in range(slab_y):
        for z in range(0, slab_z, 2):
            site = y * slab_z + z
            plans = []
            for here in (site, site + 1):
                plan = [(1, here, 0, here)]
                if y > 0:
                    plan.append((2, here - slab_z, 1, here - slab_z))
                if here > y * slab_z:
                    plan.append((3, here - 1, 2, here - 1))
                plans.append(plan)
            matrices = [[matrix(d, s) for _, _, d, s in plan] for plan in plans]
            for i, here in enumerate((site, site + 1)):
                source = v_ref[y, z + i]
                part = jnp.dot(
                    jnp.concatenate(matrices[i], axis=0), stack(source), preferred_element_type=jnp.float32
                )
                tiles = source.astype(jnp.float32).reshape(rows // 8, 8, width)
                below, above = pltpu.roll(tiles, 7, 1), pltpu.roll(tiles, 1, 1)
                swapped = jnp.where(is_real, -below, above).reshape(rows, width)
                image = waves[0] * source.astype(jnp.float32) + waves[1] * swapped
                turned[y, z + i] = swapped.astype(jnp.bfloat16)
                right[at(here), :width] = image.astype(jnp.bfloat16)
                for j, (operator, target, _, _) in enumerate(plans[i]):
                    put(target, operator, part[j * rows : (j + 1) * rows])
        right[at(y * slab_z + slab_z - 1), 3 * width : 4 * width] = jnp.zeros((rows, width), jnp.bfloat16)
        right[at(y * slab_z + slab_z - 1), 5 * width : 6 * width] = jnp.zeros((rows, width), jnp.bfloat16)
    last = pl.ds((slab_y - 1) * slab_z * rows, slab_z * rows)
    right[last, 2 * width : 3 * width] = jnp.zeros((slab_z * rows, width), jnp.bfloat16)
    right[last, 4 * width : 5 * width] = jnp.zeros((slab_z * rows, width), jnp.bfloat16)
    left = jnp.concatenate(
        [v_ref[...].reshape(sites * rows, width), turned[...].reshape(sites * rows, width)], axis=1
    )
    both = lax.dot_general(
        left, right[...], (((0,), (0,)), ((), ())), preferred_element_type=jnp.float32
    )
    total[:, : 2 * width] = both[:, : 2 * width]
    total[:, 2 * width :] = both[:, 2 * width : 4 * width] + both[:, 4 * width :]


def edge_kernel(scale, face_z, face_y, total, v_ref, turned, out, sums):
    width = face_y.shape[1]

    def product(parts, face):
        first = jnp.concatenate([part.reshape(face.shape) for part in parts], axis=1)
        return lax.dot_general(
            first, face[...], (((0,), (0,)), ((), ())), preferred_element_type=jnp.float32
        )

    extra = {
        2: product((v_ref[0], turned[0]), face_y),
        3: product((v_ref[:, 0], turned[:, 0]), face_z),
    }
    for operator in range(4):
        both = total[:, operator * width : (operator + 1) * width]
        if operator in extra:
            both = both - extra[operator]
        real, imag = both[:width], both[width:]
        if operator < 2:
            factor = scale if operator == 0 else 0.5 * scale
            real, imag = real * factor, imag * factor
        else:
            real, imag = (real - real.T) * (0.5 * scale), (imag + imag.T) * (0.5 * scale)
        sums[pl.ds(2 * operator, width, stride=8), :] = real
        sums[pl.ds(2 * operator + 1, width, stride=8), :] = imag
    out[...] = sums[...].astype(jnp.bfloat16)


def sum_kernel(gathered, out):
    pairs = gathered.shape[0] // 16
    sums = [jnp.zeros((16, gathered.shape[1]), jnp.float32) for _ in range(4)]
    for i in range(pairs):
        sums[i % 4] = sums[i % 4] + gathered[pl.ds(16 * i, 16), :].astype(jnp.float32)
    both = (sums[0] + sums[1]) + (sums[2] + sums[3])
    out[...] = both[:8] + both[8:]


def shifted(block, axis):
    size = lax.axis_size(axis)
    return lax.ppermute(block, axis, [(i, (i + 1) % size) for i in range(size)])


def per_device(eigenvectors, gauge_links):
    _, slab_y, slab_z, count, _, _, width = eigenvectors.shape
    rows = 6 * count
    sites = slab_y * slab_z
    scale = (6.0 * count * slab_y * lax.axis_size("gy") * slab_z * lax.axis_size("gz")) ** (-0.5)
    field = jnp.transpose(eigenvectors[0], (0, 1, 2, 4, 3, 5)).reshape(slab_y, slab_z, rows, width)
    links = gauge_links.reshape(54, sites, count)
    waves, spread, masks = constants(count)
    inputs = (field, links, waves, spread, masks)
    face_y, face_z, *inputs = pl.pallas_call(
        functools.partial(first_kernel, slab_y, slab_z, count),
        out_shape=[
            pltpu.VMEM((slab_z * rows, width), jnp.bfloat16),
            pltpu.VMEM((slab_y * rows, width), jnp.bfloat16),
            *(pltpu.VMEM(each.shape, each.dtype) for each in inputs),
        ],
        in_specs=[pl.BlockSpec(memory_space=pltpu.HBM)] * 5,
        scratch_shapes=[
            pltpu.VMEM((3 * sites, 128), jnp.float32),
            pltpu.VMEM((2 * 8 * 24, 128), jnp.float32),
            pltpu.VMEM((2 * slab_y * 24, 128), jnp.float32),
            pltpu.SemaphoreType.DMA((10,)),
        ],
        compiler_params=pltpu.CompilerParams(vmem_limit_bytes=24 * 1024 * 1024),
        cost_estimate=pl.CostEstimate(flops=2_000_000_000, bytes_accessed=600_000, transcendentals=0),
    )(*(pltpu.with_memory_space_constraint(each, pltpu.HBM) for each in inputs))
    face_y = shifted(face_y, "gy")
    face_z = shifted(face_z, "gz")
    total, turned = pl.pallas_call(
        functools.partial(local_kernel, slab_y, slab_z, count),
        out_shape=[
            jax.ShapeDtypeStruct((2 * width, 4 * width), jnp.float32),
            jax.ShapeDtypeStruct((slab_y, slab_z, rows, width), jnp.bfloat16),
        ],
        scratch_shapes=[
            pltpu.VMEM((8 * sites * 24, 128), jnp.float32),
            pltpu.VMEM((sites * rows, 6 * width), jnp.bfloat16),
        ],
        compiler_params=pltpu.CompilerParams(vmem_limit_bytes=32 * 1024 * 1024),
        cost_estimate=pl.CostEstimate(flops=5_000_000_000, bytes_accessed=4_000_000, transcendentals=0),
    )(*inputs)
    partial = pl.pallas_call(
        functools.partial(edge_kernel, scale),
        out_shape=jax.ShapeDtypeStruct((8 * width, width), jnp.bfloat16),
        scratch_shapes=[pltpu.VMEM((8 * width, width), jnp.float32)],
        compiler_params=pltpu.CompilerParams(vmem_limit_bytes=16 * 1024 * 1024),
    )(face_z, face_y, total, inputs[0], turned)
    gathered = lax.all_to_all(partial.reshape(width, 8, width), ("gy", "gz"), 0, 0, tiled=True)
    mine = pl.pallas_call(
        sum_kernel,
        out_shape=jax.ShapeDtypeStruct((8, width), jnp.float32),
        compiler_params=pltpu.CompilerParams(vmem_limit_bytes=8 * 1024 * 1024),
    )(gathered.reshape(8 * width, width))
    return mine.reshape(1, 1, 4, 2, width)


def solution(mesh):
    placed = (
        P(None, "gy", "gz", None, None, None, None),
        P(None, None, None, None, None, "gy", "gz", None),
    )
    return jax.shard_map(
        per_device,
        mesh=mesh,
        in_specs=placed,
        out_specs=P(("gy", "gz"), None, None, None, None),
        check_vma=False,
    )
```

```python
import functools

import jax
import jax.numpy as jnp
import ml_dtypes
import numpy as np
from jax import lax
from jax.experimental import pallas as pl
from jax.experimental.pallas import tpu as pltpu
from jax.sharding import PartitionSpec as P

BF16 = ml_dtypes.bfloat16


def row_at(x, colour, part):
    return (x * 3 + colour) * 2 + part


def constants(count):
    rows = 6 * count
    angles = np.arange(count, dtype=np.float32) * np.float32(2.0 * np.pi / count)
    waves = np.repeat(np.stack([np.cos(angles), -np.sin(angles)]), 6, axis=1)
    waves = np.broadcast_to(waves[..., None], (2, rows, 128)).astype(np.float32)
    spread = np.zeros((2, 128, 2, 128), np.float32)
    masks = np.zeros((3, rows, 128), np.float32)
    for shift in range(2):
        for x in range(count):
            there = (x + shift) % count
            for colour in range(3):
                for part in range(2):
                    for to_part in range(2):
                        lane = ((part ^ to_part) * 3 + colour) * count + x
                        sign = -1.0 if (part, to_part) == (0, 1) else 1.0
                        spread[shift, lane, part, row_at(there, colour, to_part)] = sign
            masks[shift, 6 * x : 6 * x + 6, 6 * there : 6 * there + 6] = 1.0
            if shift == 1:
                masks[2, 6 * there : 6 * there + 6, 6 * x : 6 * x + 6] = -1.0
    return (
        waves,
        spread.reshape(2, 128, 256).astype(BF16),
        masks.astype(BF16),
    )


def site_rows(site, rows):
    return pl.ds(pl.multiple_of(site * rows, rows), rows)


def spread_links(flat, spread):
    high = flat.astype(jnp.bfloat16)
    low = (flat - high.astype(jnp.float32)).astype(jnp.bfloat16)
    both = jnp.concatenate([high, low], axis=0)
    both = jnp.dot(both, spread, preferred_element_type=jnp.float32)
    return both[: flat.shape[0]], both[flat.shape[0] :]


def store_coefs(coefs, base, stride, wide, sites):
    for colour in range(3):
        for part in range(2):
            for half in range(2):
                value = wide[half][colour * sites : (colour + 1) * sites, part * 128 : part * 128 + 128]
                for copy in range(4):
                    first = base + half * stride + copy * 6 + colour * 2 + part
                    coefs[pl.ds(first, sites, stride=24), :] = value


def block_matrix(coefs, start, stride, rows, mask):
    halves = []
    for half in range(2):
        value = coefs[pl.ds(pl.multiple_of(start + half * stride, 24), 24), :]
        value = jnp.concatenate([value, value], axis=0).astype(jnp.bfloat16)
        halves.append(jnp.concatenate([value] * (rows // 48), axis=0) * mask)
    return jnp.concatenate(halves, axis=1)


def apply(matrices, source):
    rows, width = source.shape
    padding = jnp.zeros((128 - rows, width), source.dtype)
    return jnp.dot(
        jnp.concatenate(matrices, axis=0),
        jnp.concatenate([source, padding, source, padding], axis=0),
        preferred_element_type=jnp.float32,
    ).astype(jnp.bfloat16)


def back_links(links, direction, first, number, count):
    flat = []
    for other in range(3):
        pieces = []
        for part in range(2):
            for colour in range(3):
                piece = links[((direction * 2 + part) * 3 + colour) * 3 + other, pl.ds(first, number), :]
                pieces.append(-piece if part else piece)
        pieces.append(jnp.zeros((number, 128 - 6 * count), jnp.float32))
        flat.append(jnp.concatenate(pieces, axis=1))
    return jnp.concatenate(flat, axis=0)


def first_kernel(
    slab_y, slab_z, count, v_hbm, links_hbm, waves_hbm, spread_hbm, masks_hbm,
    face_y, face_z, v_ref, links, waves, spread, masks, flat, coefs_y, coefs_z, sems,
):
    sites = slab_y * slab_z
    mine, others = pl.ds(0, slab_y - 1), pl.ds(0, slab_z - 1)
    along_x, along_y, along_z = (pl.ds(18 * i, 18) for i in range(3))
    whole = (slice(None),)
    pairs = [
        (links_hbm, links, (along_z,)),
        (spread_hbm, spread, whole),
        (links_hbm, links, (along_y, pl.ds(sites - 8, 8))),
        (masks_hbm, masks, whole),
        (v_hbm, v_ref, (slab_y - 1,)),
        (v_hbm, v_ref, (mine, slab_z - 1)),
        (links_hbm, links, (along_x,)),
        (links_hbm, links, (along_y, pl.ds(0, sites - 8))),
        (v_hbm, v_ref, (mine, others)),
        (waves_hbm, waves, whole),
    ]
    moves = [
        pltpu.make_async_copy(source.at[where], target.at[where], sems.at[i])
        for i, (source, target, where) in enumerate(pairs)
    ]
    for move in moves:
        move.start()
    rows = 6 * count
    for move in moves[:3]:
        move.wait()
    flat[...] = back_links(links, 2, 0, sites, count)
    edge = flat[pl.ds(slab_z - 1, 3 * slab_y, stride=slab_z), :]
    edge = jnp.concatenate([edge, back_links(links, 1, sites - 8, 8, count)], axis=0)
    wide = spread_links(edge, spread[0])
    store_coefs(coefs_z, 0, slab_y * 24, [half[: 3 * slab_y] for half in wide], slab_y)
    store_coefs(coefs_y, 0, 8 * 24, [half[3 * slab_y :] for half in wide], 8)
    for move in moves[3:6]:
        move.wait()
    mask = masks[0]
    jobs = [(face_y, z, coefs_y, 8 - slab_z + z, v_ref[slab_y - 1, z]) for z in range(slab_z)]
    jobs += [(face_z, y, coefs_z, y, v_ref[y, slab_z - 1]) for y in range(slab_y)]
    for pair in zip(jobs[::2], jobs[1::2]):
        matrices = [block_matrix(table, at * 24, 8 * 24, rows, mask) for _, _, table, at, _ in pair]
        images = apply(matrices, jnp.concatenate([job[4] for job in pair], axis=1))
        for i, (face, at, *_) in enumerate(pair):
            width = face.shape[1]
            face[site_rows(at, rows), :] = images[i * rows : (i + 1) * rows, i * width : (i + 1) * width]
    for move in moves[6:]:
        move.wait()


def local_kernel(
    slab_y, slab_z, count, v_ref, links, waves, spread, masks, total, first_y, first_z,
    turned, coefs, right,
):
    rows = 6 * count
    sites = slab_y * slab_z
    width = v_ref.shape[-1]

    tables = []
    for direction in range(3):
        flat = []
        for colour in range(3):
            pieces = []
            for part in range(2):
                for other in range(3):
                    pieces.append(links[((direction * 2 + part) * 3 + colour) * 3 + other])
            pieces.append(jnp.zeros((sites, 128 - rows), jnp.float32))
            flat.append(jnp.concatenate(pieces, axis=1))
        tables.append(jnp.concatenate(flat, axis=0))
    tables.append(back_links(links, 0, 0, sites, count))
    wide = spread_links(tables[0], spread[1])
    store_coefs(coefs, 0, 4 * sites * 24, wide, sites)
    wide = spread_links(jnp.concatenate(tables[1:], axis=0), spread[0])
    for i in range(3):
        mine = [half[3 * sites * i : 3 * sites * (i + 1)] for half in wide]
        store_coefs(coefs, (i + 1) * sites * 24, 4 * sites * 24, mine, sites)

    mask = [masks[i] for i in range(3)]

    def matrix(direction, site):
        start, stride = (direction * sites + site) * 24, 4 * sites * 24
        if direction > 0:
            return block_matrix(coefs, start, stride, rows, mask[0])
        ahead = block_matrix(coefs, start, stride, rows, mask[1])
        return ahead + block_matrix(coefs, (3 * sites + site) * 24, stride, rows, mask[2])

    def at(site):
        return site_rows(site, rows)

    def stack(source):
        padding = jnp.zeros((128 - rows, width), source.dtype)
        return jnp.concatenate([source, padding, source, padding], axis=0)

    is_real = lax.broadcasted_iota(jnp.int32, (rows // 8, 8, width), 1) % 2 == 0

    def put(site, operator, image):
        high = image.astype(jnp.bfloat16)
        right[at(site), operator * width : (operator + 1) * width] = high
        if operator > 1:
            low = (image - high.astype(jnp.float32)).astype(jnp.bfloat16)
            right[at(site), (operator + 2) * width : (operator + 3) * width] = low

    for y in range(slab_y):
        for z in range(0, slab_z, 2):
            site = y * slab_z + z
            plans = []
            for here in (site, site + 1):
                plan = [(1, here, 0, here)]
                if y > 0:
                    plan.append((2, here - slab_z, 1, here - slab_z))
                if here > y * slab_z:
                    plan.append((3, here - 1, 2, here - 1))
                plans.append(plan)
            matrices = [[matrix(d, s) for _, _, d, s in plan] for plan in plans]
            for i, here in enumerate((site, site + 1)):
                source = v_ref[y, z + i]
                part = jnp.dot(
                    jnp.concatenate(matrices[i], axis=0), stack(source), preferred_element_type=jnp.float32
                )
                tiles = source.astype(jnp.float32).reshape(rows // 8, 8, width)
                below, above = pltpu.roll(tiles, 7, 1), pltpu.roll(tiles, 1, 1)
                swapped = jnp.where(is_real, -below, above).reshape(rows, width)
                image = waves[0] * source.astype(jnp.float32) + waves[1] * swapped
                turned[y, z + i] = swapped.astype(jnp.bfloat16)
                right[at(here), :width] = image.astype(jnp.bfloat16)
                for j, (operator, target, _, _) in enumerate(plans[i]):
                    put(target, operator, part[j * rows : (j + 1) * rows])
        right[at(y * slab_z + slab_z - 1), 3 * width : 4 * width] = jnp.zeros((rows, width), jnp.bfloat16)
        right[at(y * slab_z + slab_z - 1), 5 * width : 6 * width] = jnp.zeros((rows, width), jnp.bfloat16)
    last = pl.ds((slab_y - 1) * slab_z * rows, slab_z * rows)
    right[last, 2 * width : 3 * width] = jnp.zeros((slab_z * rows, width), jnp.bfloat16)
    right[last, 4 * width : 5 * width] = jnp.zeros((slab_z * rows, width), jnp.bfloat16)
    for first, of in ((first_y, (0,)), (first_z, (slice(None), 0))):
        parts = [ref[of].reshape(-1, width) for ref in (v_ref, turned)]
        first[...] = jnp.concatenate(parts, axis=1).T
    left = jnp.concatenate(
        [v_ref[...].reshape(sites * rows, width), turned[...].reshape(sites * rows, width)], axis=1
    )
    both = lax.dot_general(
        left, right[...], (((0,), (0,)), ((), ())), preferred_element_type=jnp.float32
    )
    total[:, : 2 * width] = both[:, : 2 * width]
    total[:, 2 * width :] = both[:, 2 * width : 4 * width] + both[:, 4 * width :]


def edge_kernel(scale, face_z, face_y, total, first_y, first_z, out, sums):
    width = face_y.shape[1]

    def product(first, face):
        return jnp.dot(first[...], face[...], preferred_element_type=jnp.float32)

    extra = {2: product(first_y, face_y), 3: product(first_z, face_z)}
    for operator in range(4):
        both = total[:, operator * width : (operator + 1) * width]
        if operator in extra:
            both = both - extra[operator]
        real, imag = both[:width], both[width:]
        if operator < 2:
            factor = scale if operator == 0 else 0.5 * scale
            real, imag = real * factor, imag * factor
        else:
            real, imag = (real - real.T) * (0.5 * scale), (imag + imag.T) * (0.5 * scale)
        sums[pl.ds(2 * operator, width, stride=8), :] = real
        sums[pl.ds(2 * operator + 1, width, stride=8), :] = imag
    out[...] = sums[...].astype(jnp.bfloat16)


def sum_kernel(gathered, out):
    pairs = gathered.shape[0] // 16
    sums = [jnp.zeros((16, gathered.shape[1]), jnp.float32) for _ in range(4)]
    for i in range(pairs):
        sums[i % 4] = sums[i % 4] + gathered[pl.ds(16 * i, 16), :].astype(jnp.float32)
    both = (sums[0] + sums[1]) + (sums[2] + sums[3])
    out[...] = both[:8] + both[8:]


def shifted(block, axis):
    size = lax.axis_size(axis)
    return lax.ppermute(block, axis, [(i, (i + 1) % size) for i in range(size)])


def per_device(eigenvectors, gauge_links):
    _, slab_y, slab_z, count, _, _, width = eigenvectors.shape
    rows = 6 * count
    sites = slab_y * slab_z
    scale = (6.0 * count * slab_y * lax.axis_size("gy") * slab_z * lax.axis_size("gz")) ** (-0.5)
    field = jnp.transpose(eigenvectors[0], (0, 1, 2, 4, 3, 5)).reshape(slab_y, slab_z, rows, width)
    links = gauge_links.reshape(54, sites, count)
    waves, spread, masks = constants(count)
    inputs = (field, links, waves, spread, masks)
    face_y, face_z, *inputs = pl.pallas_call(
        functools.partial(first_kernel, slab_y, slab_z, count),
        out_shape=[
            pltpu.VMEM((slab_z * rows, width), jnp.bfloat16),
            pltpu.VMEM((slab_y * rows, width), jnp.bfloat16),
            *(pltpu.VMEM(each.shape, each.dtype) for each in inputs),
        ],
        in_specs=[pl.BlockSpec(memory_space=pltpu.HBM)] * 5,
        scratch_shapes=[
            pltpu.VMEM((3 * sites, 128), jnp.float32),
            pltpu.VMEM((2 * 8 * 24, 128), jnp.float32),
            pltpu.VMEM((2 * slab_y * 24, 128), jnp.float32),
            pltpu.SemaphoreType.DMA((10,)),
        ],
        compiler_params=pltpu.CompilerParams(vmem_limit_bytes=24 * 1024 * 1024),
        cost_estimate=pl.CostEstimate(flops=2_000_000_000, bytes_accessed=600_000, transcendentals=0),
    )(*(pltpu.with_memory_space_constraint(each, pltpu.HBM) for each in inputs))
    face_y = shifted(face_y, "gy")
    face_z = shifted(face_z, "gz")
    total, first_y, first_z = pl.pallas_call(
        functools.partial(local_kernel, slab_y, slab_z, count),
        out_shape=[
            jax.ShapeDtypeStruct((2 * width, 4 * width), jnp.float32),
            jax.ShapeDtypeStruct((2 * width, slab_z * rows), jnp.bfloat16),
            jax.ShapeDtypeStruct((2 * width, slab_y * rows), jnp.bfloat16),
        ],
        scratch_shapes=[
            pltpu.VMEM((slab_y, slab_z, rows, width), jnp.bfloat16),
            pltpu.VMEM((8 * sites * 24, 128), jnp.float32),
            pltpu.VMEM((sites * rows, 6 * width), jnp.bfloat16),
        ],
        compiler_params=pltpu.CompilerParams(vmem_limit_bytes=32 * 1024 * 1024),
        cost_estimate=pl.CostEstimate(flops=5_000_000_000, bytes_accessed=4_000_000, transcendentals=0),
    )(*inputs)
    partial = pl.pallas_call(
        functools.partial(edge_kernel, scale),
        out_shape=jax.ShapeDtypeStruct((8 * width, width), jnp.bfloat16),
        scratch_shapes=[pltpu.VMEM((8 * width, width), jnp.float32)],
        compiler_params=pltpu.CompilerParams(vmem_limit_bytes=16 * 1024 * 1024),
    )(face_z, face_y, total, first_y, first_z)
    gathered = lax.all_to_all(partial.reshape(width, 8, width), ("gy", "gz"), 0, 0, tiled=True)
    mine = pl.pallas_call(
        sum_kernel,
        out_shape=jax.ShapeDtypeStruct((8, width), jnp.float32),
        compiler_params=pltpu.CompilerParams(vmem_limit_bytes=8 * 1024 * 1024),
    )(gathered.reshape(8 * width, width))
    return mine.reshape(1, 1, 4, 2, width)


def solution(mesh):
    placed = (
        P(None, "gy", "gz", None, None, None, None),
        P(None, None, None, None, None, "gy", "gz", None),
    )
    return jax.shard_map(
        per_device,
        mesh=mesh,
        in_specs=placed,
        out_specs=P(("gy", "gz"), None, None, None, None),
        check_vma=False,
    )
```

```python
import functools

import jax
import jax.numpy as jnp
import ml_dtypes
import numpy as np
from jax import lax
from jax.experimental import pallas as pl
from jax.experimental.pallas import tpu as pltpu
from jax.sharding import PartitionSpec as P

BF16 = ml_dtypes.bfloat16


def row_at(x, colour, part):
    return (x * 3 + colour) * 2 + part


def constants(count):
    rows = 6 * count
    angles = np.arange(count, dtype=np.float32) * np.float32(2.0 * np.pi / count)
    waves = np.repeat(np.stack([np.cos(angles), -np.sin(angles)]), 6, axis=1)
    waves = np.broadcast_to(waves[..., None], (2, rows, 128)).astype(np.float32)
    spread = np.zeros((2, 128, 2, 128), np.float32)
    masks = np.zeros((3, rows, 128), np.float32)
    for shift in range(2):
        for x in range(count):
            there = (x + shift) % count
            for colour in range(3):
                for part in range(2):
                    for to_part in range(2):
                        lane = ((part ^ to_part) * 3 + colour) * count + x
                        sign = -1.0 if (part, to_part) == (0, 1) else 1.0
                        spread[shift, lane, part, row_at(there, colour, to_part)] = sign
            masks[shift, 6 * x : 6 * x + 6, 6 * there : 6 * there + 6] = 1.0
            if shift == 1:
                masks[2, 6 * there : 6 * there + 6, 6 * x : 6 * x + 6] = -1.0
    return (
        waves,
        spread.reshape(2, 128, 256).astype(BF16),
        masks.astype(BF16),
    )


def site_rows(site, rows):
    return pl.ds(pl.multiple_of(site * rows, rows), rows)


def spread_links(flat, spread):
    high = flat.astype(jnp.bfloat16)
    low = (flat - high.astype(jnp.float32)).astype(jnp.bfloat16)
    both = jnp.concatenate([high, low], axis=0)
    both = jnp.dot(both, spread, preferred_element_type=jnp.float32)
    return both[: flat.shape[0]], both[flat.shape[0] :]


def store_coefs(coefs, base, stride, wide, sites):
    for colour in range(3):
        for part in range(2):
            for half in range(2):
                value = wide[half][colour * sites : (colour + 1) * sites, part * 128 : part * 128 + 128]
                for copy in range(4):
                    first = base + half * stride + copy * 6 + colour * 2 + part
                    coefs[pl.ds(first, sites, stride=24), :] = value


def block_matrix(coefs, start, stride, rows, mask):
    halves = []
    for half in range(2):
        value = coefs[pl.ds(pl.multiple_of(start + half * stride, 24), 24), :]
        value = jnp.concatenate([value, value], axis=0).astype(jnp.bfloat16)
        halves.append(jnp.concatenate([value] * (rows // 48), axis=0) * mask)
    return jnp.concatenate(halves, axis=1)


def apply(matrices, source):
    rows, width = source.shape
    padding = jnp.zeros((128 - rows, width), source.dtype)
    return jnp.dot(
        jnp.concatenate(matrices, axis=0),
        jnp.concatenate([source, padding, source, padding], axis=0),
        preferred_element_type=jnp.float32,
    ).astype(jnp.bfloat16)


def back_links(links, direction, first, number, count):
    flat = []
    for other in range(3):
        pieces = []
        for part in range(2):
            for colour in range(3):
                piece = links[((direction * 2 + part) * 3 + colour) * 3 + other, pl.ds(first, number), :]
                pieces.append(-piece if part else piece)
        pieces.append(jnp.zeros((number, 128 - 6 * count), jnp.float32))
        flat.append(jnp.concatenate(pieces, axis=1))
    return jnp.concatenate(flat, axis=0)


def first_kernel(
    slab_y, slab_z, count, v_hbm, links_hbm, waves_hbm, spread_hbm, masks_hbm,
    face_y, face_z, v_ref, links, waves, spread, masks, flat, coefs_y, coefs_z, sems,
):
    sites = slab_y * slab_z
    mine, others = pl.ds(0, slab_y - 1), pl.ds(0, slab_z - 1)
    along_x, along_y, along_z = (pl.ds(18 * i, 18) for i in range(3))
    whole = (slice(None),)
    pairs = [
        (links_hbm, links, (along_z,)),
        (spread_hbm, spread, whole),
        (links_hbm, links, (along_y, pl.ds(sites - 8, 8))),
        (masks_hbm, masks, whole),
        (v_hbm, v_ref, (slab_y - 1,)),
        (v_hbm, v_ref, (mine, slab_z - 1)),
        (links_hbm, links, (along_x,)),
        (links_hbm, links, (along_y, pl.ds(0, sites - 8))),
        (v_hbm, v_ref, (mine, others)),
        (waves_hbm, waves, whole),
    ]
    moves = [
        pltpu.make_async_copy(source.at[where], target.at[where], sems.at[i])
        for i, (source, target, where) in enumerate(pairs)
    ]
    for i, move in enumerate(moves):
        move.start(priority=0 if i < 6 else 1)
    rows = 6 * count
    for move in moves[:3]:
        move.wait()
    flat[...] = back_links(links, 2, 0, sites, count)
    edge = flat[pl.ds(slab_z - 1, 3 * slab_y, stride=slab_z), :]
    edge = jnp.concatenate([edge, back_links(links, 1, sites - 8, 8, count)], axis=0)
    wide = spread_links(edge, spread[0])
    store_coefs(coefs_z, 0, slab_y * 24, [half[: 3 * slab_y] for half in wide], slab_y)
    store_coefs(coefs_y, 0, 8 * 24, [half[3 * slab_y :] for half in wide], 8)
    for move in moves[3:6]:
        move.wait()
    mask = masks[0]
    jobs = [(face_y, z, coefs_y, 8 - slab_z + z, v_ref[slab_y - 1, z]) for z in range(slab_z)]
    jobs += [(face_z, y, coefs_z, y, v_ref[y, slab_z - 1]) for y in range(slab_y)]
    for pair in zip(jobs[::2], jobs[1::2]):
        matrices = [block_matrix(table, at * 24, 8 * 24, rows, mask) for _, _, table, at, _ in pair]
        images = apply(matrices, jnp.concatenate([job[4] for job in pair], axis=1))
        for i, (face, at, *_) in enumerate(pair):
            width = face.shape[1]
            face[site_rows(at, rows), :] = images[i * rows : (i + 1) * rows, i * width : (i + 1) * width]
    for move in moves[6:]:
        move.wait()


def local_kernel(
    slab_y, slab_z, count, v_ref, links, waves, spread, masks, total, first_y, first_z,
    turned, coefs, right,
):
    rows = 6 * count
    sites = slab_y * slab_z
    width = v_ref.shape[-1]

    tables = []
    for direction in range(3):
        flat = []
        for colour in range(3):
            pieces = []
            for part in range(2):
                for other in range(3):
                    pieces.append(links[((direction * 2 + part) * 3 + colour) * 3 + other])
            pieces.append(jnp.zeros((sites, 128 - rows), jnp.float32))
            flat.append(jnp.concatenate(pieces, axis=1))
        tables.append(jnp.concatenate(flat, axis=0))
    tables.append(back_links(links, 0, 0, sites, count))
    wide = spread_links(tables[0], spread[1])
    store_coefs(coefs, 0, 4 * sites * 24, wide, sites)
    wide = spread_links(jnp.concatenate(tables[1:], axis=0), spread[0])
    for i in range(3):
        mine = [half[3 * sites * i : 3 * sites * (i + 1)] for half in wide]
        store_coefs(coefs, (i + 1) * sites * 24, 4 * sites * 24, mine, sites)

    mask = [masks[i] for i in range(3)]

    def matrix(direction, site):
        start, stride = (direction * sites + site) * 24, 4 * sites * 24
        if direction > 0:
            return block_matrix(coefs, start, stride, rows, mask[0])
        ahead = block_matrix(coefs, start, stride, rows, mask[1])
        return ahead + block_matrix(coefs, (3 * sites + site) * 24, stride, rows, mask[2])

    def at(site):
        return site_rows(site, rows)

    def stack(source):
        padding = jnp.zeros((128 - rows, width), source.dtype)
        return jnp.concatenate([source, padding, source, padding], axis=0)

    is_real = lax.broadcasted_iota(jnp.int32, (rows // 8, 8, width), 1) % 2 == 0

    def put(site, operator, image):
        high = image.astype(jnp.bfloat16)
        right[at(site), operator * width : (operator + 1) * width] = high
        if operator > 1:
            low = (image - high.astype(jnp.float32)).astype(jnp.bfloat16)
            right[at(site), (operator + 2) * width : (operator + 3) * width] = low

    for y in range(slab_y):
        for z in range(0, slab_z, 2):
            site = y * slab_z + z
            plans = []
            for here in (site, site + 1):
                plan = [(1, here, 0, here)]
                if y > 0:
                    plan.append((2, here - slab_z, 1, here - slab_z))
                if here > y * slab_z:
                    plan.append((3, here - 1, 2, here - 1))
                plans.append(plan)
            matrices = [[matrix(d, s) for _, _, d, s in plan] for plan in plans]
            for i, here in enumerate((site, site + 1)):
                source = v_ref[y, z + i]
                part = jnp.dot(
                    jnp.concatenate(matrices[i], axis=0), stack(source), preferred_element_type=jnp.float32
                )
                tiles = source.astype(jnp.float32).reshape(rows // 8, 8, width)
                below, above = pltpu.roll(tiles, 7, 1), pltpu.roll(tiles, 1, 1)
                swapped = jnp.where(is_real, -below, above).reshape(rows, width)
                image = waves[0] * source.astype(jnp.float32) + waves[1] * swapped
                turned[y, z + i] = swapped.astype(jnp.bfloat16)
                right[at(here), :width] = image.astype(jnp.bfloat16)
                for j, (operator, target, _, _) in enumerate(plans[i]):
                    put(target, operator, part[j * rows : (j + 1) * rows])
        right[at(y * slab_z + slab_z - 1), 3 * width : 4 * width] = jnp.zeros((rows, width), jnp.bfloat16)
        right[at(y * slab_z + slab_z - 1), 5 * width : 6 * width] = jnp.zeros((rows, width), jnp.bfloat16)
    last = pl.ds((slab_y - 1) * slab_z * rows, slab_z * rows)
    right[last, 2 * width : 3 * width] = jnp.zeros((slab_z * rows, width), jnp.bfloat16)
    right[last, 4 * width : 5 * width] = jnp.zeros((slab_z * rows, width), jnp.bfloat16)
    for first, of in ((first_y, (0,)), (first_z, (slice(None), 0))):
        parts = [ref[of].reshape(-1, width) for ref in (v_ref, turned)]
        first[...] = jnp.concatenate(parts, axis=1).T
    left = jnp.concatenate(
        [v_ref[...].reshape(sites * rows, width), turned[...].reshape(sites * rows, width)], axis=1
    )
    both = lax.dot_general(
        left, right[...], (((0,), (0,)), ((), ())), preferred_element_type=jnp.float32
    )
    total[:, : 2 * width] = both[:, : 2 * width]
    total[:, 2 * width :] = both[:, 2 * width : 4 * width] + both[:, 4 * width :]


def edge_kernel(scale, face_z, face_y, total, first_y, first_z, out, sums):
    width = face_y.shape[1]

    def product(first, face):
        return jnp.dot(first[...], face[...], preferred_element_type=jnp.float32)

    extra = {2: product(first_y, face_y), 3: product(first_z, face_z)}
    for operator in range(4):
        both = total[:, operator * width : (operator + 1) * width]
        if operator in extra:
            both = both - extra[operator]
        real, imag = both[:width], both[width:]
        if operator < 2:
            factor = scale if operator == 0 else 0.5 * scale
            real, imag = real * factor, imag * factor
        else:
            real, imag = (real - real.T) * (0.5 * scale), (imag + imag.T) * (0.5 * scale)
        sums[pl.ds(2 * operator, width, stride=8), :] = real
        sums[pl.ds(2 * operator + 1, width, stride=8), :] = imag
    out[...] = sums[...].astype(jnp.bfloat16)


def sum_kernel(gathered, out):
    pairs = gathered.shape[0] // 16
    sums = [jnp.zeros((16, gathered.shape[1]), jnp.float32) for _ in range(4)]
    for i in range(pairs):
        sums[i % 4] = sums[i % 4] + gathered[pl.ds(16 * i, 16), :].astype(jnp.float32)
    both = (sums[0] + sums[1]) + (sums[2] + sums[3])
    out[...] = both[:8] + both[8:]


def shifted(block, axis):
    size = lax.axis_size(axis)
    return lax.ppermute(block, axis, [(i, (i + 1) % size) for i in range(size)])


def per_device(eigenvectors, gauge_links):
    _, slab_y, slab_z, count, _, _, width = eigenvectors.shape
    rows = 6 * count
    sites = slab_y * slab_z
    scale = (6.0 * count * slab_y * lax.axis_size("gy") * slab_z * lax.axis_size("gz")) ** (-0.5)
    field = jnp.transpose(eigenvectors[0], (0, 1, 2, 4, 3, 5)).reshape(slab_y, slab_z, rows, width)
    links = gauge_links.reshape(54, sites, count)
    waves, spread, masks = constants(count)
    inputs = (field, links, waves, spread, masks)
    face_y, face_z, *inputs = pl.pallas_call(
        functools.partial(first_kernel, slab_y, slab_z, count),
        out_shape=[
            pltpu.VMEM((slab_z * rows, width), jnp.bfloat16),
            pltpu.VMEM((slab_y * rows, width), jnp.bfloat16),
            *(pltpu.VMEM(each.shape, each.dtype) for each in inputs),
        ],
        in_specs=[pl.BlockSpec(memory_space=pltpu.HBM)] * 5,
        scratch_shapes=[
            pltpu.VMEM((3 * sites, 128), jnp.float32),
            pltpu.VMEM((2 * 8 * 24, 128), jnp.float32),
            pltpu.VMEM((2 * slab_y * 24, 128), jnp.float32),
            pltpu.SemaphoreType.DMA((10,)),
        ],
        compiler_params=pltpu.CompilerParams(vmem_limit_bytes=24 * 1024 * 1024),
        cost_estimate=pl.CostEstimate(flops=2_000_000_000, bytes_accessed=600_000, transcendentals=0),
    )(*(pltpu.with_memory_space_constraint(each, pltpu.HBM) for each in inputs))
    face_y = shifted(face_y, "gy")
    face_z = shifted(face_z, "gz")
    total, first_y, first_z = pl.pallas_call(
        functools.partial(local_kernel, slab_y, slab_z, count),
        out_shape=[
            jax.ShapeDtypeStruct((2 * width, 4 * width), jnp.float32),
            jax.ShapeDtypeStruct((2 * width, slab_z * rows), jnp.bfloat16),
            jax.ShapeDtypeStruct((2 * width, slab_y * rows), jnp.bfloat16),
        ],
        scratch_shapes=[
            pltpu.VMEM((slab_y, slab_z, rows, width), jnp.bfloat16),
            pltpu.VMEM((8 * sites * 24, 128), jnp.float32),
            pltpu.VMEM((sites * rows, 6 * width), jnp.bfloat16),
        ],
        compiler_params=pltpu.CompilerParams(vmem_limit_bytes=32 * 1024 * 1024),
        cost_estimate=pl.CostEstimate(flops=5_000_000_000, bytes_accessed=4_000_000, transcendentals=0),
    )(*inputs)
    partial = pl.pallas_call(
        functools.partial(edge_kernel, scale),
        out_shape=jax.ShapeDtypeStruct((8 * width, width), jnp.bfloat16),
        scratch_shapes=[pltpu.VMEM((8 * width, width), jnp.float32)],
        compiler_params=pltpu.CompilerParams(vmem_limit_bytes=16 * 1024 * 1024),
    )(face_z, face_y, total, first_y, first_z)
    gathered = lax.all_to_all(partial.reshape(width, 8, width), ("gy", "gz"), 0, 0, tiled=True)
    mine = pl.pallas_call(
        sum_kernel,
        out_shape=jax.ShapeDtypeStruct((8, width), jnp.float32),
        compiler_params=pltpu.CompilerParams(vmem_limit_bytes=8 * 1024 * 1024),
    )(gathered.reshape(8 * width, width))
    return mine.reshape(1, 1, 4, 2, width)


def solution(mesh):
    placed = (
        P(None, "gy", "gz", None, None, None, None),
        P(None, None, None, None, None, "gy", "gz", None),
    )
    return jax.shard_map(
        per_device,
        mesh=mesh,
        in_specs=placed,
        out_specs=P(("gy", "gz"), None, None, None, None),
        check_vma=False,
    )
```

```python
import functools

import jax
import jax.numpy as jnp
import ml_dtypes
import numpy as np
from jax import lax
from jax.experimental import pallas as pl
from jax.experimental.pallas import tpu as pltpu
from jax.sharding import PartitionSpec as P

BF16 = ml_dtypes.bfloat16


def row_at(x, colour, part):
    return (x * 3 + colour) * 2 + part


def constants(count):
    rows = 6 * count
    angles = np.arange(count, dtype=np.float32) * np.float32(2.0 * np.pi / count)
    waves = np.repeat(np.stack([np.cos(angles), -np.sin(angles)]), 6, axis=1)
    waves = np.broadcast_to(waves[..., None], (2, rows, 128)).astype(np.float32)
    spread = np.zeros((2, 128, 2, 128), np.float32)
    masks = np.zeros((3, rows, 128), np.float32)
    for shift in range(2):
        for x in range(count):
            there = (x + shift) % count
            for colour in range(3):
                for part in range(2):
                    for to_part in range(2):
                        lane = ((part ^ to_part) * 3 + colour) * count + x
                        sign = -1.0 if (part, to_part) == (0, 1) else 1.0
                        spread[shift, lane, part, row_at(there, colour, to_part)] = sign
            masks[shift, 6 * x : 6 * x + 6, 6 * there : 6 * there + 6] = 1.0
            if shift == 1:
                masks[2, 6 * there : 6 * there + 6, 6 * x : 6 * x + 6] = -1.0
    return (
        waves,
        spread.reshape(2, 128, 256).astype(BF16),
        masks.astype(BF16),
    )


def site_rows(site, rows):
    return pl.ds(pl.multiple_of(site * rows, rows), rows)


def spread_links(flat, spread):
    high = flat.astype(jnp.bfloat16)
    low = (flat - high.astype(jnp.float32)).astype(jnp.bfloat16)
    both = jnp.concatenate([high, low], axis=0)
    both = jnp.dot(both, spread, preferred_element_type=jnp.float32)
    return both[: flat.shape[0]], both[flat.shape[0] :]


def store_coefs(coefs, base, stride, wide, sites):
    for colour in range(3):
        for part in range(2):
            for half in range(2):
                value = wide[half][colour * sites : (colour + 1) * sites, part * 128 : part * 128 + 128]
                for copy in range(4):
                    first = base + half * stride + copy * 6 + colour * 2 + part
                    coefs[pl.ds(first, sites, stride=24), :] = value


def block_matrix(coefs, start, stride, rows, mask):
    halves = []
    for half in range(2):
        value = coefs[pl.ds(pl.multiple_of(start + half * stride, 24), 24), :]
        value = jnp.concatenate([value, value], axis=0).astype(jnp.bfloat16)
        halves.append(jnp.concatenate([value] * (rows // 48), axis=0) * mask)
    return jnp.concatenate(halves, axis=1)


def apply(matrices, source):
    rows, width = source.shape
    padding = jnp.zeros((128 - rows, width), source.dtype)
    return jnp.dot(
        jnp.concatenate(matrices, axis=0),
        jnp.concatenate([source, padding, source, padding], axis=0),
        preferred_element_type=jnp.float32,
    ).astype(jnp.bfloat16)


def back_links(links, direction, first, number, count):
    flat = []
    for other in range(3):
        pieces = []
        for part in range(2):
            for colour in range(3):
                piece = links[((direction * 2 + part) * 3 + colour) * 3 + other, pl.ds(first, number), :]
                pieces.append(-piece if part else piece)
        pieces.append(jnp.zeros((number, 128 - 6 * count), jnp.float32))
        flat.append(jnp.concatenate(pieces, axis=1))
    return jnp.concatenate(flat, axis=0)


def first_kernel(
    slab_y, slab_z, count, v_hbm, links_hbm, waves_hbm, spread_hbm, masks_hbm,
    face_y, face_z, v_ref, links, waves, spread, masks, flat, coefs_y, coefs_z, sems,
):
    sites = slab_y * slab_z
    mine, others = pl.ds(0, slab_y - 1), pl.ds(0, slab_z - 1)
    along_x, along_y, along_z = (pl.ds(18 * i, 18) for i in range(3))
    whole = (slice(None),)
    pairs = [
        (links_hbm, links, (along_z,)),
        (spread_hbm, spread, whole),
        (links_hbm, links, (along_y, pl.ds(sites - 8, 8))),
        (masks_hbm, masks, whole),
        (v_hbm, v_ref, (slab_y - 1,)),
        (v_hbm, v_ref, (mine, slab_z - 1)),
        (links_hbm, links, (along_x,)),
        (links_hbm, links, (along_y, pl.ds(0, sites - 8))),
        (v_hbm, v_ref, (mine, others)),
        (waves_hbm, waves, whole),
    ]
    moves = [
        pltpu.make_async_copy(source.at[where], target.at[where], sems.at[i])
        for i, (source, target, where) in enumerate(pairs)
    ]
    for move in moves:
        move.start()
    rows = 6 * count
    for move in moves[:3]:
        move.wait()
    flat[...] = back_links(links, 2, 0, sites, count)
    edge = flat[pl.ds(slab_z - 1, 3 * slab_y, stride=slab_z), :]
    edge = jnp.concatenate([edge, back_links(links, 1, sites - 8, 8, count)], axis=0)
    wide = spread_links(edge, spread[0])
    store_coefs(coefs_z, 0, slab_y * 24, [half[: 3 * slab_y] for half in wide], slab_y)
    store_coefs(coefs_y, 0, 8 * 24, [half[3 * slab_y :] for half in wide], 8)
    for move in moves[3:6]:
        move.wait()
    mask = masks[0]
    jobs = [(face_y, z, coefs_y, 8 - slab_z + z, v_ref[slab_y - 1, z]) for z in range(slab_z)]
    jobs += [(face_z, y, coefs_z, y, v_ref[y, slab_z - 1]) for y in range(slab_y)]
    for pair in zip(jobs[::2], jobs[1::2]):
        matrices = [block_matrix(table, at * 24, 8 * 24, rows, mask) for _, _, table, at, _ in pair]
        images = apply(matrices, jnp.concatenate([job[4] for job in pair], axis=1))
        for i, (face, at, *_) in enumerate(pair):
            width = face.shape[1]
            face[site_rows(at, rows), :] = images[i * rows : (i + 1) * rows, i * width : (i + 1) * width]
    for move in moves[6:]:
        move.wait()


def local_kernel(
    slab_y, slab_z, count, v_ref, links, waves, spread, masks, total, first_y, first_z,
    turned, coefs, right,
):
    rows = 6 * count
    sites = slab_y * slab_z
    width = v_ref.shape[-1]

    tables = []
    for direction in range(3):
        flat = []
        for colour in range(3):
            pieces = []
            for part in range(2):
                for other in range(3):
                    pieces.append(links[((direction * 2 + part) * 3 + colour) * 3 + other])
            pieces.append(jnp.zeros((sites, 128 - rows), jnp.float32))
            flat.append(jnp.concatenate(pieces, axis=1))
        tables.append(jnp.concatenate(flat, axis=0))
    tables.append(back_links(links, 0, 0, sites, count))
    wide = spread_links(tables[0], spread[1])
    store_coefs(coefs, 0, 4 * sites * 24, wide, sites)
    wide = spread_links(jnp.concatenate(tables[1:], axis=0), spread[0])
    for i in range(3):
        mine = [half[3 * sites * i : 3 * sites * (i + 1)] for half in wide]
        store_coefs(coefs, (i + 1) * sites * 24, 4 * sites * 24, mine, sites)

    mask = [masks[i] for i in range(3)]

    def matrix(direction, site):
        start, stride = (direction * sites + site) * 24, 4 * sites * 24
        if direction > 0:
            return block_matrix(coefs, start, stride, rows, mask[0])
        ahead = block_matrix(coefs, start, stride, rows, mask[1])
        return ahead + block_matrix(coefs, (3 * sites + site) * 24, stride, rows, mask[2])

    def at(site):
        return site_rows(site, rows)

    def stack(source):
        padding = jnp.zeros((128 - rows, width), source.dtype)
        return jnp.concatenate([source, padding, source, padding], axis=0)

    is_real = lax.broadcasted_iota(jnp.int32, (rows // 8, 8, width), 1) % 2 == 0

    def put(site, operator, image):
        high = image.astype(jnp.bfloat16)
        right[at(site), operator * width : (operator + 1) * width] = high
        if operator > 1:
            low = (image - high.astype(jnp.float32)).astype(jnp.bfloat16)
            right[at(site), (operator + 2) * width : (operator + 3) * width] = low

    for y in range(slab_y):
        for z in range(0, slab_z, 2):
            site = y * slab_z + z
            plans = []
            for here in (site, site + 1):
                plan = [(1, here, 0, here)]
                if y > 0:
                    plan.append((2, here - slab_z, 1, here - slab_z))
                if here > y * slab_z:
                    plan.append((3, here - 1, 2, here - 1))
                plans.append(plan)
            matrices = [[matrix(d, s) for _, _, d, s in plan] for plan in plans]
            for i, here in enumerate((site, site + 1)):
                source = v_ref[y, z + i]
                part = jnp.dot(
                    jnp.concatenate(matrices[i], axis=0), stack(source), preferred_element_type=jnp.float32
                )
                tiles = source.astype(jnp.float32).reshape(rows // 8, 8, width)
                below, above = pltpu.roll(tiles, 7, 1), pltpu.roll(tiles, 1, 1)
                swapped = jnp.where(is_real, -below, above).reshape(rows, width)
                image = waves[0] * source.astype(jnp.float32) + waves[1] * swapped
                turned[y, z + i] = swapped.astype(jnp.bfloat16)
                right[at(here), :width] = image.astype(jnp.bfloat16)
                for j, (operator, target, _, _) in enumerate(plans[i]):
                    put(target, operator, part[j * rows : (j + 1) * rows])
        right[at(y * slab_z + slab_z - 1), 3 * width : 4 * width] = jnp.zeros((rows, width), jnp.bfloat16)
        right[at(y * slab_z + slab_z - 1), 5 * width : 6 * width] = jnp.zeros((rows, width), jnp.bfloat16)
    last = pl.ds((slab_y - 1) * slab_z * rows, slab_z * rows)
    right[last, 2 * width : 3 * width] = jnp.zeros((slab_z * rows, width), jnp.bfloat16)
    right[last, 4 * width : 5 * width] = jnp.zeros((slab_z * rows, width), jnp.bfloat16)
    for first, of in ((first_y, (0,)), (first_z, (slice(None), 0))):
        parts = [ref[of].reshape(-1, width) for ref in (v_ref, turned)]
        first[...] = jnp.concatenate(parts, axis=1).T
    left = jnp.concatenate(
        [v_ref[...].reshape(sites * rows, width), turned[...].reshape(sites * rows, width)], axis=1
    )
    both = lax.dot_general(
        left, right[...], (((0,), (0,)), ((), ())), preferred_element_type=jnp.float32
    )
    total[:, : 2 * width] = both[:, : 2 * width]
    total[:, 2 * width :] = both[:, 2 * width : 4 * width] + both[:, 4 * width :]


def edge_kernel(scale, face_z, face_y, total, first_y, first_z, out, sums):
    width = face_y.shape[1]

    def product(first, face):
        return jnp.dot(first[...], face[...], preferred_element_type=jnp.float32)

    extra = {2: product(first_y, face_y), 3: product(first_z, face_z)}
    for operator in range(4):
        both = total[:, operator * width : (operator + 1) * width]
        if operator in extra:
            both = both - extra[operator]
        real, imag = both[:width], both[width:]
        if operator < 2:
            factor = scale if operator == 0 else 0.5 * scale
            real, imag = real * factor, imag * factor
        else:
            real, imag = (real - real.T) * (0.5 * scale), (imag + imag.T) * (0.5 * scale)
        sums[pl.ds(2 * operator, width, stride=8), :] = real
        sums[pl.ds(2 * operator + 1, width, stride=8), :] = imag
    out[...] = sums[...].astype(jnp.bfloat16)


def sum_kernel(gathered, out):
    pairs = gathered.shape[0] // 16
    sums = [jnp.zeros((16, gathered.shape[1]), jnp.float32) for _ in range(4)]
    for i in range(pairs):
        sums[i % 4] = sums[i % 4] + gathered[pl.ds(16 * i, 16), :].astype(jnp.float32)
    both = (sums[0] + sums[1]) + (sums[2] + sums[3])
    out[...] = both[:8] + both[8:]


def shifted(block, axis):
    size = lax.axis_size(axis)
    return lax.ppermute(block, axis, [(i, (i + 1) % size) for i in range(size)])


def per_device(eigenvectors, gauge_links):
    _, slab_y, slab_z, count, _, _, width = eigenvectors.shape
    rows = 6 * count
    sites = slab_y * slab_z
    scale = (6.0 * count * slab_y * lax.axis_size("gy") * slab_z * lax.axis_size("gz")) ** (-0.5)
    field = jnp.transpose(eigenvectors[0], (0, 1, 2, 4, 3, 5)).reshape(slab_y, slab_z, rows, width)
    links = gauge_links.reshape(54, sites, count)
    waves, spread, masks = constants(count)
    inputs = (field, links, waves, spread, masks)
    face_y, face_z, *inputs = pl.pallas_call(
        functools.partial(first_kernel, slab_y, slab_z, count),
        out_shape=[
            pltpu.VMEM((slab_z * rows, width), jnp.bfloat16),
            pltpu.VMEM((slab_y * rows, width), jnp.bfloat16),
            *(pltpu.VMEM(each.shape, each.dtype) for each in inputs),
        ],
        in_specs=[pl.BlockSpec(memory_space=pltpu.HBM)] * 5,
        scratch_shapes=[
            pltpu.VMEM((3 * sites, 128), jnp.float32),
            pltpu.VMEM((2 * 8 * 24, 128), jnp.float32),
            pltpu.VMEM((2 * slab_y * 24, 128), jnp.float32),
            pltpu.SemaphoreType.DMA((10,)),
        ],
        compiler_params=pltpu.CompilerParams(vmem_limit_bytes=24 * 1024 * 1024),
        cost_estimate=pl.CostEstimate(flops=2_000_000_000, bytes_accessed=600_000, transcendentals=0),
    )(*(pltpu.with_memory_space_constraint(each, pltpu.HBM) for each in inputs))
    face_y = shifted(face_y, "gy")
    face_z = shifted(face_z, "gz")
    total, first_y, first_z = pl.pallas_call(
        functools.partial(local_kernel, slab_y, slab_z, count),
        out_shape=[
            jax.ShapeDtypeStruct((2 * width, 4 * width), jnp.float32),
            jax.ShapeDtypeStruct((2 * width, slab_z * rows), jnp.bfloat16),
            jax.ShapeDtypeStruct((2 * width, slab_y * rows), jnp.bfloat16),
        ],
        scratch_shapes=[
            pltpu.VMEM((slab_y, slab_z, rows, width), jnp.bfloat16),
            pltpu.VMEM((8 * sites * 24, 128), jnp.float32),
            pltpu.VMEM((sites * rows, 6 * width), jnp.bfloat16),
        ],
        compiler_params=pltpu.CompilerParams(vmem_limit_bytes=32 * 1024 * 1024),
        cost_estimate=pl.CostEstimate(flops=500_000_000, bytes_accessed=1_000_000, transcendentals=0),
    )(*inputs)
    partial = pl.pallas_call(
        functools.partial(edge_kernel, scale),
        out_shape=jax.ShapeDtypeStruct((8 * width, width), jnp.bfloat16),
        scratch_shapes=[pltpu.VMEM((8 * width, width), jnp.float32)],
        compiler_params=pltpu.CompilerParams(vmem_limit_bytes=16 * 1024 * 1024),
    )(face_z, face_y, total, first_y, first_z)
    gathered = lax.all_to_all(partial.reshape(width, 8, width), ("gy", "gz"), 0, 0, tiled=True)
    mine = pl.pallas_call(
        sum_kernel,
        out_shape=jax.ShapeDtypeStruct((8, width), jnp.float32),
        compiler_params=pltpu.CompilerParams(vmem_limit_bytes=8 * 1024 * 1024),
    )(gathered.reshape(8 * width, width))
    return mine.reshape(1, 1, 4, 2, width)


def solution(mesh):
    placed = (
        P(None, "gy", "gz", None, None, None, None),
        P(None, None, None, None, None, "gy", "gz", None),
    )
    return jax.shard_map(
        per_device,
        mesh=mesh,
        in_specs=placed,
        out_specs=P(("gy", "gz"), None, None, None, None),
        check_vma=False,
    )
```
